512 devices in a mesh: item: 16 (over y_lo, x), cent: 32 (over z, y_hi, core).
Axes of the slice: x: 4, y: 8 (y_hi: 2, y_lo: 4; y = y_hi * 4 + y_lo), z: 8, core: 2. Of those that a mesh axis runs over, the one named last changes fastest.
Arguments:
- vectors: bfloat16 [12288, 1024], P('item'), may hold values from -256 to 256, as said below
- centroids: bfloat16 [32768, 1024], P('cent'), may hold values from -6 to 6, as said below
Outputs:
- centroids_next: bfloat16 [32768, 1024], P(('cent', 'item'))
- log_norm: float32 [12288], P('item')
The draws below stay inside these ranges and needn't reach their ends.
Inputs may be any that keep to these rules, and one draw needn't show every extreme that they name: vectors hold finite values. `centroids`: centroid entries are independent.
All inputs are finite; a program needn't handle non-finite values.
Results may differ from the reference program's by a relative error of at most 0.0085.
Values may be sent and summed in bfloat16 or wider, within the bound.
A program may use at most 64 MiB of HBM per device.

```python
import math
import jax
import jax.numpy as jnp
from jax import lax

D = 1024
NV_DEV = 768
ITERS = 2
NV = 12288
K = 32768
N_ITEM = 16


BETA = 3.0


def centroid_table(key):
    base = jax.random.normal(jax.random.fold_in(key, 7), (K, D), jnp.float32)
    return jnp.clip(base, -6.0, 6.0)


def draw_centroids(key, part):
    return centroid_table(key).astype(jnp.bfloat16)


def aligned_rows(key):
    table = centroid_table(key)
    keys = jax.random.split(jax.random.fold_in(key, 23), 3)
    first = jax.random.randint(keys[0], (NV,), 0, K)
    second = (first + 1 + jax.random.randint(keys[1], (NV,), 0, K - 1)) % K
    level = 120.0 + 80.0 * (jnp.arange(NV) // 64 % 3).astype(jnp.float32)
    strength = 0.5 + level / (BETA * math.sqrt(D))
    delta = jax.random.uniform(keys[2], (NV,), jnp.float32, 1.5, 2.5)
    near_one = table[first]
    near_two = table[second]
    norm_one = jnp.sum(near_one * near_one, axis=1)
    norm_two = jnp.sum(near_two * near_two, axis=1)
    cross = jnp.sum(near_one * near_two, axis=1)
    scale = BETA / math.sqrt(D)
    weight_two = (strength * norm_one - 0.5 * norm_one - strength * cross + 0.5 * norm_two - delta / scale) / (norm_two - cross)
    return strength[:, None] * near_one + weight_two[:, None] * near_two


def draw_vectors(key, part):
    noise_key = jax.random.fold_in(key, 19)
    base = jnp.clip(jax.random.normal(noise_key, (NV, D), jnp.float32), -6.0, 6.0)
    picked = jnp.arange(NV) % 64 == 0
    result = jnp.where(picked[:, None], aligned_rows(key), base)
    return jnp.clip(result, -256.0, 256.0).astype(jnp.bfloat16)


def setup_inputs(seed: int = 0) -> dict:
    splits = jax.random.split(jax.random.key(seed), 3)
    vectors = draw_vectors(jax.random.fold_in(splits[2], 71), 0)
    centroids = draw_centroids(jax.random.fold_in(splits[2], 71), 0)
    return {"vectors": vectors, "centroids": centroids}


BETA = 3.0

def reference(vectors, centroids):
    current = centroids
    scale = BETA / math.sqrt(D)
    blocks = vectors.reshape(N_ITEM, NV_DEV, D)
    log_rows = jnp.zeros((N_ITEM, NV_DEV), jnp.float32)
    for step in range(ITERS):
        sqnorm = lax.optimization_barrier(jnp.sum(jnp.square(current.astype(jnp.float32)), axis=1))

        def one_block(carry, block):
            sums, mass = carry
            raw = jnp.dot(block, current.T, preferred_element_type=jnp.float32)
            logits = scale * (raw - 0.5 * sqnorm[None, :])
            peak = lax.optimization_barrier(jnp.max(logits, axis=1))
            expo = jnp.exp(logits - peak[:, None])
            total = lax.optimization_barrier(jnp.sum(expo, axis=1))
            resp = (expo / total[:, None]).astype(jnp.bfloat16)
            term = jnp.dot(resp.T, block, preferred_element_type=jnp.float32)
            term = lax.optimization_barrier(term.astype(jnp.bfloat16)).astype(jnp.float32)
            mass = mass + lax.optimization_barrier(jnp.sum(resp.astype(jnp.float32), axis=0))
            return ((sums + term, mass), peak + jnp.log(total))
        start = (jnp.zeros((K, D), jnp.float32), jnp.zeros((K,), jnp.float32))
        (sums, mass), log_rows = lax.scan(one_block, start, blocks)
        current = ((sums + current.astype(jnp.float32)) / (mass + 1.0)[:, None]).astype(jnp.bfloat16)
    return (current, log_rows.reshape(NV))
```

```python
import functools
import math

import jax
import jax.numpy as jnp
from jax import lax
from jax.experimental import pallas as pl
from jax.experimental.pallas import tpu as pltpu
from jax.sharding import PartitionSpec as P

MESH = pl.DeviceIdType.MESH
F32, BF16 = jnp.float32, jnp.bfloat16
BETA = 3.0
NX, NY, NZ, YLO = 4, 8, 8, 4
NV, D = 768, 1024
ROWS = 256
OWN = 64
NC = 4
W = D // NC
CH = 64
HALF = NV // 2
SCALE = BETA / math.sqrt(D)


def nt(a, b):
    return lax.dot_general(a, b, (((1,), (1,)), ((), ())), preferred_element_type=F32)


def merge(pairs):
    peak = functools.reduce(jnp.maximum, [p for p, _ in pairs])
    return peak, sum(t * jnp.exp(p - peak) for p, t in pairs)


def local_stats(logits):
    peak = jnp.max(logits, axis=0, keepdims=True)
    return peak, jnp.sum(jnp.exp(logits - peak), axis=0, keepdims=True)


def half_sq(rows):
    wide = rows.astype(F32)
    return 0.5 * jnp.sum(wide * wide, axis=1, keepdims=True)


def kernel(
    vec, cen, out, logn,
    vall, cvm, cnew, lbuf, resp, wbuf, rbuf, mbuf, mcol,
    core1, zst1, yst1, core2, yst2, zst2, fst2,
    in_sem, ys, yr, zs, zr, cs, cr,
    st_s, st_r, z_s, z_r, y_s, y_r, rs_s, rs_r, ag_s, ag_r, m_s, m_r,
):
    item, cent = lax.axis_index("item"), lax.axis_index("cent")
    x, q = lax.rem(item, NX), item // NX
    z, yhi, c = cent // 4, lax.rem(cent // 2, 2), lax.rem(cent, 2)
    y = yhi * YLO + q

    def dev(dx=0, dy=0, dz=0, dc=0):
        x2, y2 = lax.rem(x + dx + NX, NX), lax.rem(y + dy + NY, NY)
        z2, c2 = lax.rem(z + dz + NZ, NZ), lax.rem(c + dc, 2)
        return {"item": lax.rem(y2, YLO) * NX + x2, "cent": z2 * 4 + (y2 // YLO) * 2 + c2}

    started = []

    def send(src, dst, s, r, **to):
        copy = pltpu.make_async_remote_copy(
            src_ref=src, dst_ref=dst, send_sem=s, recv_sem=r, device_id=dev(**to), device_id_type=MESH
        )
        copy.start()
        started.append(copy)
        return copy

    mine = pl.ds(pl.multiple_of(q * NV, NV), NV)
    load_v = pltpu.make_async_copy(vec, vall.at[mine], in_sem.at[0])
    load_c = pltpu.make_async_copy(cen, cvm, in_sem.at[1])
    load_v.start()
    load_c.start()
    barrier = pltpu.get_barrier_semaphore()
    peers = [dict(dc=1)]
    peers += [dict(dx=k) for k in range(1, NX)]
    peers += [dict(dy=k) for k in range(1, NY)] + [dict(dz=k) for k in range(1, NZ)]
    for to in peers:
        pl.semaphore_signal(barrier, inc=1, device_id=dev(**to), device_id_type=MESH)
    load_v.wait()
    load_c.wait()

    def score(k, carry):
        rows = cvm[pl.ds(pl.multiple_of(k * ROWS, ROWS), ROWS), :]
        logits = SCALE * (nt(rows, vall[mine, :]) - half_sq(rows))
        return merge([carry, local_stats(logits)])

    peak, total = lax.fori_loop(
        0, 4, score, (jnp.full((1, NV), -3.0e38, F32), jnp.zeros((1, NV), F32))
    )
    core1[0, 0:1, :] = peak
    core1[0, 1:2, :] = total

    pl.semaphore_wait(barrier, len(peers))

    par = lax.rem(z, 2)
    kp, ko = 2 * par, 2 - 2 * par

    def piece(block, k):
        b = lax.rem(q + block + YLO, YLO)
        start = b * NV + c * HALF + k * CH
        return vall.at[pl.ds(pl.multiple_of(start, CH), CH)]

    def ysend(up, slot, block, k):
        side = 0 if up else 1
        part = piece(block, k)
        return send(part, part, ys.at[side, slot], yr.at[side, slot], dy=1 if up else -1)

    def zsend(up, slot, block, k):
        side = 0 if up else 1
        part = piece(block, k)
        return send(part, part, zs.at[side, slot], zr.at[side, slot], dz=1 if up else -1)

    passed = []

    def cross(block, k):
        part = piece(block, k)
        n = len(passed)
        passed.append(send(part, part, cs.at[n], cr.at[n], dc=1))

    up, down = [None] * 6, [None] * 6
    zup, zdown = [None] * 3, [None] * 3
    up[0], down[0] = ysend(True, 0, 0, kp), ysend(False, 0, 0, kp + 1)
    up[1], down[1] = ysend(True, 1, 0, kp + 1), ysend(False, 1, 0, kp)

    other = send(core1.at[0], core1.at[1], st_s.at[0], st_r.at[0], dc=1)
    other.wait_recv()
    peak, total = merge([(core1[k, 0:1, :], core1[k, 1:2, :]) for k in range(2)])
    zst1[z, 0:1, :] = peak
    zst1[z, 1:2, :] = total
    zall = [send(zst1.at[z], zst1.at[z], z_s.at[0, k], z_r.at[0, k], dz=k) for k in range(1, NZ)]

    up[0].wait_recv()
    down[0].wait_recv()
    up[2], down[2] = ysend(True, 2, -1, kp), ysend(False, 2, 1, kp + 1)
    zup[0], zdown[0] = zsend(True, 0, -1, kp), zsend(False, 0, 1, kp + 1)
    up[3], down[3] = ysend(True, 3, 0, 4), ysend(False, 3, 0, 5)
    up[4], down[4] = ysend(True, 4, 0, 5), ysend(False, 4, 0, 4)
    cross(-1, kp)
    cross(1, kp + 1)

    for copy in zall:
        copy.wait_recv()
    peak, total = merge([(zst1[k, 0:1, :], zst1[k, 1:2, :]) for k in range(NZ)])
    yst1[y, 0:1, :] = peak
    yst1[y, 1:2, :] = total
    yall = [send(yst1.at[y], yst1.at[y], y_s.at[0, k], y_r.at[0, k], dy=k) for k in range(1, NY)]

    up[1].wait_recv()
    down[1].wait_recv()
    zup[1], zdown[1] = zsend(True, 1, 1, kp), zsend(False, 1, -1, kp + 1)
    cross(-1, kp + 1)
    cross(1, kp)
    up[2].wait_recv()
    down[2].wait_recv()
    zup[2], zdown[2] = zsend(True, 2, 2, kp), zsend(False, 2, 2, kp + 1)
    cross(2, kp)
    cross(2, kp + 1)
    zup[0].wait_recv()
    zdown[0].wait_recv()
    cross(-1, ko)
    cross(1, ko + 1)
    up[3].wait_recv()
    down[3].wait_recv()
    up[5], down[5] = ysend(True, 5, -1, 4), ysend(False, 5, 1, 5)
    cross(-1, 4)
    cross(1, 5)
    zup[1].wait_recv()
    zdown[1].wait_recv()
    cross(1, ko)
    cross(-1, ko + 1)

    for copy in yall:
        copy.wait_recv()
    crow = pl.ds(pl.multiple_of(q * ROWS, ROWS), ROWS)
    rows = cvm[crow, :]
    half = half_sq(rows)

    def respond(block):
        b = lax.rem(q + block, YLO)
        peak, total = merge([(yst1[b + k, 0:1, :], yst1[b + k, 1:2, :]) for k in (0, YLO)])
        part = vall[pl.ds(pl.multiple_of(b * NV, NV), NV), :]
        logits = SCALE * (nt(rows, part) - half)
        resp[b] = (jnp.exp(logits - peak) * (1.0 / total)).astype(BF16)

    respond(0)
    up[4].wait_recv()
    down[4].wait_recv()
    cross(-1, 5)
    cross(1, 4)
    zup[2].wait_recv()
    zdown[2].wait_recv()
    cross(2, ko)
    cross(2, ko + 1)
    up[5].wait_recv()
    down[5].wait_recv()
    cross(2, 4)
    cross(2, 5)
    for copy in passed:
        copy.wait_recv()
    for block in (1, 2, 3):
        respond(block)

    own = pl.ds(pl.multiple_of(q * ROWS + x * OWN, OWN), OWN)
    own64 = pl.ds(pl.multiple_of(x * OWN, OWN), OWN)

    def reduce(it, old, emit):
        mass = sum(jnp.sum(resp[b].astype(F32), axis=1, keepdims=True) for b in range(YLO))
        mbuf[it, x] = jnp.transpose(jnp.broadcast_to(mass, (ROWS, 128)))[0:1, :]
        mall = [
            send(mbuf.at[it, x], mbuf.at[it, x], m_s.at[it, k], m_r.at[it, k], dx=k) for k in range(1, NX)
        ]
        sent = []
        for n in range(NC):
            cols = slice(n * W, (n + 1) * W)
            part = sum(
                jnp.dot(resp[b], vall[b * NV : (b + 1) * NV, cols], preferred_element_type=F32)
                for b in range(YLO)
            )
            wbuf[it, n] = part.astype(BF16).reshape(NX, OWN, W)
            rbuf[it, n, 0] = wbuf[it, n, x]
            sent.append([
                send(
                    wbuf.at[it, n, lax.rem(x + k, NX)], rbuf.at[it, n, k],
                    rs_s.at[it, n, k], rs_r.at[it, n, k], dx=k,
                )
                for k in (2, 1, 3)
            ])
        for copy in mall:
            copy.wait_recv()
        row = sum(mbuf[it, k] for k in range(NX))
        mcol[...] = jnp.transpose(jnp.broadcast_to(row, (128, ROWS)))
        div = mcol[own64, 0:1] + 1.0
        for n in range(NC):
            for copy in sent[n]:
                copy.wait_recv()
            sums = sum(rbuf[it, n, k].astype(F32) for k in range(NX))
            emit(n, ((sums + old(n).astype(F32)) / div).astype(BF16))

    gathered = []

    def spread(n, fresh):
        cnew[n, x] = fresh
        gathered.append([
            send(cnew.at[n, x], cnew.at[n, x], ag_s.at[n, k], ag_r.at[n, k], dx=k) for k in (2, 1, 3)
        ])

    reduce(0, lambda n: cvm[own, n * W : (n + 1) * W], spread)

    half = jnp.zeros((ROWS, 1), F32)
    for n in range(NC):
        for copy in gathered[n]:
            copy.wait_recv()
        rows = cnew[n].reshape(ROWS, W)
        half = half + half_sq(rows)
        for b in range(YLO):
            term = nt(rows, vall[b * NV : (b + 1) * NV, n * W : (n + 1) * W])
            lbuf[b] = term if n == 0 else lbuf[b] + term

    for b in range(YLO):
        logits = SCALE * (lbuf[b] - half)
        lbuf[b] = logits
        peak, total = local_stats(logits)
        core2[0, b, 0:1, :] = peak
        core2[0, b, 1:2, :] = total

    pair = pl.ds(2 * c, 2)
    theirs = pl.ds(2 - 2 * c, 2)
    other = send(core2.at[0, theirs], core2.at[1, theirs], st_s.at[1], st_r.at[1], dc=1)
    other.wait_recv()
    for j in range(2):
        b = 2 * c + j
        peak, total = merge([(core2[k, b, 0:1, :], core2[k, b, 1:2, :]) for k in range(2)])
        yst2[y, j, 0:1, :] = peak
        yst2[y, j, 1:2, :] = total
    yall = [send(yst2.at[y], yst2.at[y], y_s.at[1, k], y_r.at[1, k], dy=k) for k in range(1, NY)]
    for copy in yall:
        copy.wait_recv()
    for j in range(2):
        peak, total = merge([(yst2[k, j, 0:1, :], yst2[k, j, 1:2, :]) for k in range(NY)])
        zst2[z, j, 0:1, :] = peak
        zst2[z, j, 1:2, :] = total
    zall = [send(zst2.at[z], zst2.at[z], z_s.at[1, k], z_r.at[1, k], dz=k) for k in range(1, NZ)]
    for copy in zall:
        copy.wait_recv()
    for j in range(2):
        peak, total = merge([(zst2[k, j, 0:1, :], zst2[k, j, 1:2, :]) for k in range(NZ)])
        fst2[2 * c + j, 0:1, :] = peak
        fst2[2 * c + j, 1:2, :] = total
    other = send(fst2.at[pair], fst2.at[pair], st_s.at[2], st_r.at[2], dc=1)
    other.wait_recv()

    for b in range(YLO):
        peak, total = fst2[b, 0:1, :], fst2[b, 1:2, :]
        resp[b] = (jnp.exp(lbuf[b] - peak) * (1.0 / total)).astype(BF16)
    norm = fst2[q, 0:1, :] + jnp.log(fst2[q, 1:2, :])
    for k in range(NV // 128):
        logn[k : k + 1, :] = norm[:, k * 128 : (k + 1) * 128]

    def finish(n, fresh):
        out[:, n * W : (n + 1) * W] = fresh

    reduce(1, lambda n: cnew[n, x], finish)

    for copy in started:
        copy.wait_send()


def shards(vectors, centroids):
    dma = pltpu.SemaphoreType.DMA
    result, log_norm = pl.pallas_call(
        kernel,
        out_shape=(
            jax.ShapeDtypeStruct((OWN, D), BF16),
            jax.ShapeDtypeStruct((NV // 128, 128), F32),
        ),
        in_specs=[pl.BlockSpec(memory_space=pl.ANY)] * 2,
        out_specs=(pl.BlockSpec(memory_space=pltpu.VMEM),) * 2,
        scratch_shapes=[
            pltpu.VMEM((YLO * NV, D), BF16),
            pltpu.VMEM((4 * ROWS, D), BF16),
            pltpu.VMEM((NC, NX, OWN, W), BF16),
            pltpu.VMEM((YLO, ROWS, NV), F32),
            pltpu.VMEM((YLO, ROWS, NV), BF16),
            pltpu.VMEM((2, NC, NX, OWN, W), BF16),
            pltpu.VMEM((2, NC, NX, OWN, W), BF16),
            pltpu.VMEM((2, NX, 1, ROWS), F32),
            pltpu.VMEM((ROWS, 128), F32),
            pltpu.VMEM((2, 2, NV), F32),
            pltpu.VMEM((NZ, 2, NV), F32),
            pltpu.VMEM((NY, 2, NV), F32),
            pltpu.VMEM((2, YLO, 2, NV), F32),
            pltpu.VMEM((NY, 2, 2, NV), F32),
            pltpu.VMEM((NZ, 2, 2, NV), F32),
            pltpu.VMEM((YLO, 2, NV), F32),
            dma((2,)),
            dma((2, 6)), dma((2, 6)), dma((2, 3)), dma((2, 3)), dma((18,)), dma((18,)),
            dma((3,)), dma((3,)), dma((2, NZ)), dma((2, NZ)), dma((2, NY)), dma((2, NY)),
            dma((2, NC, NX)), dma((2, NC, NX)), dma((NC, NX)), dma((NC, NX)),
            dma((2, NX)), dma((2, NX)),
        ],
        compiler_params=pltpu.CompilerParams(
            collective_id=0, has_side_effects=True, vmem_limit_bytes=48 * 2**20
        ),
    )(vectors, centroids)
    return result, log_norm.reshape(NV)


def solution(mesh):
    in_specs = (P("item", None), P("cent", None))
    out_specs = (P(("cent", "item"), None), P("item"))
    return jax.shard_map(shards, mesh=mesh, in_specs=in_specs, out_specs=out_specs, check_vma=False)
```

```python
import functools
import math

import jax
import jax.numpy as jnp
from jax import lax
from jax.experimental import pallas as pl
from jax.experimental.pallas import tpu as pltpu
from jax.sharding import PartitionSpec as P

MESH = pl.DeviceIdType.MESH
F32, BF16 = jnp.float32, jnp.bfloat16
BETA = 3.0
NX, NY, NZ, YLO = 4, 8, 8, 4
NV, D = 768, 1024
ROWS = 256
OWN = 64
NC = 4
W = D // NC
HALF = NV // 2
PART, REST = 80, 32
GATHER = 2 * (3 * PART + 3 * REST + 3 * PART) + 3 * HALF
SEMS = 47
SCALE = BETA / math.sqrt(D)


def nt(a, b):
    return lax.dot_general(a, b, (((1,), (1,)), ((), ())), preferred_element_type=F32)


def merge(pairs):
    peak = functools.reduce(jnp.maximum, [p for p, _ in pairs])
    return peak, sum(t * jnp.exp(p - peak) for p, t in pairs)


def local_stats(logits):
    peak = jnp.max(logits, axis=0, keepdims=True)
    return peak, jnp.sum(jnp.exp(logits - peak), axis=0, keepdims=True)


def half_sq(rows):
    wide = rows.astype(F32)
    return 0.5 * jnp.sum(wide * wide, axis=1, keepdims=True)


def kernel(
    vec, cen, out, logn,
    vall, cvm, cnew, lbuf, resp, wbuf, rbuf, mbuf, mcol,
    core1, zst1, yst1, core2, st2, fst2, sem,
):
    item, cent = lax.axis_index("item"), lax.axis_index("cent")
    x, q = lax.rem(item, NX), item // NX
    z, yhi, c = cent // 4, lax.rem(cent // 2, 2), lax.rem(cent, 2)
    y = yhi * YLO + q
    names = {}

    def sem_of(name):
        return sem.at[names.setdefault(name, len(names))]

    def dev(dx=0, dy=0, dz=0, dc=0):
        x2, y2 = lax.rem(x + dx + NX, NX), lax.rem(y + dy + NY, NY)
        z2, c2 = lax.rem(z + dz + NZ, NZ), lax.rem(c + dc, 2)
        return {"item": lax.rem(y2, YLO) * NX + x2, "cent": z2 * 4 + (y2 // YLO) * 2 + c2}

    def send(src, dst, group, arrived, **to):
        pltpu.make_async_remote_copy(
            src_ref=src, dst_ref=dst, send_sem=sem_of("s" + group), recv_sem=sem_of("r" + arrived),
            device_id=dev(**to), device_id_type=MESH,
        ).start()

    def wait(like, name):
        pltpu.make_async_copy(like, like, sem_of(name)).wait()

    barrier = pltpu.get_barrier_semaphore()
    peers = [dict(dc=1)]
    peers += [dict(dy=k) for k in range(1, NY)] + [dict(dz=k) for k in range(1, NZ)]
    peers += [dict(dx=k) for k in range(1, NX)]
    for to in peers:
        pl.semaphore_signal(barrier, inc=1, device_id=dev(**to), device_id_type=MESH)
    mine = pl.ds(pl.multiple_of(q * NV, NV), NV)
    load_v = pltpu.make_async_copy(vec, vall.at[mine], sem_of("load_v"))
    load_c = pltpu.make_async_copy(cen, cvm, sem_of("load_c"))
    load_v.start()
    load_c.start()
    pl.semaphore_wait(barrier, len(peers))

    par = lax.rem(z, 2)

    def rows_of(kind, high):
        if kind == "rest":
            return c * HALF + 4 * PART + high * REST, REST
        share = par if kind == "own" else 1 - par
        return c * HALF + (2 * share + high) * PART, PART

    def piece(block, kind, high):
        start, n = rows_of(kind, high)
        b = lax.rem(q + block + YLO, YLO)
        return vall.at[pl.ds(pl.multiple_of(b * NV + start, 16), n)]

    def first(kind, high, arrived, **to):
        start, n = rows_of(kind, high)
        send(vec.at[pl.ds(pl.multiple_of(start, 16), n)], piece(0, kind, high), "gather", arrived, **to)

    def along(block, kind, high, arrived, **to):
        part = piece(block, kind, high)
        send(part, part, "gather", arrived, **to)

    def cross(block, kind, high):
        along(block, kind, high, "far" if block == 2 else "near", dc=1)

    def landed(n, name):
        wait(vall.at[pl.ds(0, n)], name)

    first("own", 0, "A", dy=1)
    first("own", 1, "A", dy=-1)
    first("own", 1, "B", dy=1)
    first("own", 0, "B", dy=-1)
    load_v.wait()
    load_c.wait()

    def score(k, carry):
        rows = cvm[pl.ds(pl.multiple_of(k * ROWS, ROWS), ROWS), :]
        logits = SCALE * (nt(rows, vall[mine, :]) - half_sq(rows))
        lbuf[k] = logits
        return merge([carry, local_stats(logits)])

    peak, total = lax.fori_loop(
        0, 4, score, (jnp.full((1, NV), -3.0e38, F32), jnp.zeros((1, NV), F32))
    )
    core1[0, 0:1, :] = peak
    core1[0, 1:2, :] = total
    send(core1.at[0], core1.at[1], "core1", "core1", dc=1)
    wait(core1.at[1], "rcore1")
    peak, total = merge([(core1[k, 0:1, :], core1[k, 1:2, :]) for k in range(2)])
    zst1[z, 0:1, :] = peak
    zst1[z, 1:2, :] = total
    for k in range(1, NZ):
        send(zst1.at[z], zst1.at[z], "zst", "zst", dz=k)

    landed(2 * PART, "rA")
    along(-1, "own", 0, "F", dy=1)
    along(1, "own", 1, "F", dy=-1)
    along(-1, "own", 0, "Z0", dz=1)
    along(1, "own", 1, "Z0", dz=-1)
    first("rest", 0, "C", dy=1)
    first("rest", 1, "C", dy=-1)
    first("rest", 1, "D", dy=1)
    first("rest", 0, "D", dy=-1)
    cross(-1, "own", 0)
    cross(1, "own", 1)
    landed(2 * PART, "rB")
    along(1, "own", 0, "Z1", dz=1)
    along(-1, "own", 1, "Z1", dz=-1)
    cross(-1, "own", 1)
    cross(1, "own", 0)

    wait(zst1.at[pl.ds(0, NZ - 1)], "rzst")
    peak, total = merge([(zst1[k, 0:1, :], zst1[k, 1:2, :]) for k in range(NZ)])
    yst1[y, 0:1, :] = peak
    yst1[y, 1:2, :] = total
    for k in range(1, NY):
        send(yst1.at[y], yst1.at[y], "yst", "yst", dy=k)

    landed(2 * PART, "rF")
    along(2, "own", 0, "Z2", dz=1)
    along(2, "own", 1, "Z2", dz=-1)
    cross(2, "own", 0)
    cross(2, "own", 1)
    landed(2 * PART, "rZ0")
    cross(-1, "other", 0)
    cross(1, "other", 1)
    landed(2 * REST, "rC")
    along(-1, "rest", 0, "G", dy=1)
    along(1, "rest", 1, "G", dy=-1)
    cross(-1, "rest", 0)
    cross(1, "rest", 1)
    landed(2 * PART, "rZ1")
    cross(1, "other", 0)
    cross(-1, "other", 1)
    landed(2 * REST, "rD")
    cross(-1, "rest", 1)
    cross(1, "rest", 0)

    crow = pl.ds(pl.multiple_of(q * ROWS, ROWS), ROWS)
    half = half_sq(cvm[crow, :])

    def respond(block):
        b = lax.rem(q + block, YLO)
        peak, total = merge([(yst1[b + k, 0:1, :], yst1[b + k, 1:2, :]) for k in (0, YLO)])
        if block == 0:
            logits = lbuf[q]
        else:
            part = vall[pl.ds(pl.multiple_of(b * NV, NV), NV), :]
            logits = SCALE * (nt(cvm[crow, :], part) - half)
        resp[b] = (jnp.exp(logits - peak) * (1.0 / total)).astype(BF16)

    wait(yst1.at[pl.ds(0, NY - 1)], "ryst")
    respond(0)
    landed(2 * REST, "rG")
    cross(2, "rest", 0)
    cross(2, "rest", 1)
    landed(2 * HALF, "rnear")
    respond(3)
    landed(2 * PART, "rZ2")
    cross(2, "other", 0)
    cross(2, "other", 1)
    respond(1)
    landed(HALF, "rfar")
    respond(2)

    own = pl.ds(pl.multiple_of(q * ROWS + x * OWN, OWN), OWN)
    own64 = pl.ds(pl.multiple_of(x * OWN, OWN), OWN)

    def reduce(it, old, emit):
        for n in range(NC):
            cols = slice(n * W, (n + 1) * W)
            part = sum(
                jnp.dot(resp[b], vall[b * NV : (b + 1) * NV, cols], preferred_element_type=F32)
                for b in range(YLO)
            )
            wbuf[it, n] = part.astype(BF16).reshape(NX, OWN, W)
            rbuf[it, n, 0] = wbuf[it, n, x]
            for k in (2, 1, 3):
                send(
                    wbuf.at[it, n, lax.rem(x + k, NX)], rbuf.at[it, n, k],
                    f"rs{it}", f"rs{it}{n}", dx=k,
                )
            if n == 0:
                mass = sum(jnp.sum(resp[b].astype(F32), axis=1, keepdims=True) for b in range(YLO))
                mbuf[it, x] = jnp.transpose(jnp.broadcast_to(mass, (ROWS, 128)))[0:1, :]
                for k in range(1, NX):
                    send(mbuf.at[it, x], mbuf.at[it, x], f"m{it}", f"m{it}", dx=k)
        wait(mbuf.at[it, pl.ds(0, NX - 1)], f"rm{it}")
        row = sum(mbuf[it, k] for k in range(NX))
        mcol[...] = jnp.transpose(jnp.broadcast_to(row, (128, ROWS)))
        div = mcol[own64, 0:1] + 1.0
        for n in range(NC):
            wait(rbuf.at[it, n, pl.ds(1, NX - 1)], f"rrs{it}{n}")
            sums = sum(rbuf[it, n, k].astype(F32) for k in range(NX))
            emit(n, ((sums + old(n).astype(F32)) / div).astype(BF16))

    def spread(n, fresh):
        cnew[n, x] = fresh
        for k in (2, 1, 3):
            send(cnew.at[n, x], cnew.at[n, x], "ag", f"ag{n}", dx=k)

    reduce(0, lambda n: cvm[own, n * W : (n + 1) * W], spread)

    half = jnp.zeros((ROWS, 1), F32)
    for n in range(NC):
        wait(cnew.at[n, pl.ds(0, NX - 1)], f"rag{n}")
        rows = cnew[n].reshape(ROWS, W)
        half = half + half_sq(rows)
        for b in range(YLO):
            term = nt(rows, vall[b * NV : (b + 1) * NV, n * W : (n + 1) * W])
            if n > 0:
                term = lbuf[b] + term
            if n < NC - 1:
                lbuf[b] = term
            else:
                logits = SCALE * (term - half)
                peak = jnp.max(logits, axis=0, keepdims=True)
                expo = jnp.exp(logits - peak)
                lbuf[b] = expo
                core2[0, b, 0:1, :] = peak
                core2[0, b, 1:2, :] = jnp.sum(expo, axis=0, keepdims=True)

    theirs = pl.ds(2 - 2 * c, 2)
    pair = pl.ds(2 * c, 2)
    send(core2.at[0, theirs], core2.at[1, theirs], "core2", "core2", dc=1)
    wait(core2.at[1, pair], "rcore2")
    found = [
        merge([(core2[k, 2 * c + j, 0:1, :], core2[k, 2 * c + j, 1:2, :]) for k in range(2)]) for j in range(2)
    ]
    for s in range(2):
        turn = lax.rem(c + s, 2)
        at = y * (1 - turn) + z * turn
        for j in range(2):
            st2[s, at, j, 0:1, :], st2[s, at, j, 1:2, :] = found[j]
        for k in range(1, NY):
            send(st2.at[s, at], st2.at[s, at], f"st{s}", f"st{s}", dy=k * (1 - turn), dz=k * turn)
        wait(st2.at[s, pl.ds(0, NY - 1)], f"rst{s}")
        found = [merge([(st2[s, k, j, 0:1, :], st2[s, k, j, 1:2, :]) for k in range(NY)]) for j in range(2)]
    for j in range(2):
        fst2[2 * c + j, 0:1, :], fst2[2 * c + j, 1:2, :] = found[j]
    send(fst2.at[pair], fst2.at[pair], "core3", "core3", dc=1)
    wait(fst2.at[theirs], "rcore3")

    for b in range(YLO):
        peak, total = fst2[b, 0:1, :], fst2[b, 1:2, :]
        share = jnp.exp(core2[0, b, 0:1, :] - peak) * (1.0 / total)
        resp[b] = (lbuf[b] * share).astype(BF16)

    def finish(n, fresh):
        out[:, n * W : (n + 1) * W] = fresh

    reduce(1, lambda n: cnew[n, x], finish)
    norm = fst2[q, 0:1, :] + jnp.log(fst2[q, 1:2, :])
    for k in range(NV // 128):
        logn[k : k + 1, :] = norm[:, k * 128 : (k + 1) * 128]

    landed(GATHER, "sgather")
    wait(core1.at[0], "score1")
    wait(zst1.at[pl.ds(0, NZ - 1)], "szst")
    wait(yst1.at[pl.ds(0, NY - 1)], "syst")
    for it in range(2):
        wait(rbuf.at[it, pl.ds(0, NX - 1)], f"srs{it}")
        wait(mbuf.at[it, pl.ds(0, NX - 1)], f"sm{it}")
        wait(st2.at[it, pl.ds(0, NY - 1)], f"sst{it}")
    wait(cnew.at[pl.ds(0, NX - 1)], "sag")
    wait(core2.at[0, pair], "score2")
    wait(fst2.at[pair], "score3")
    assert len(names) == SEMS, len(names)


def shards(vectors, centroids):
    result, log_norm = pl.pallas_call(
        kernel,
        out_shape=(
            jax.ShapeDtypeStruct((OWN, D), BF16),
            jax.ShapeDtypeStruct((NV // 128, 128), F32),
        ),
        in_specs=[pl.BlockSpec(memory_space=pl.ANY)] * 2,
        out_specs=(pl.BlockSpec(memory_space=pltpu.VMEM),) * 2,
        scratch_shapes=[
            pltpu.VMEM((YLO * NV, D), BF16),
            pltpu.VMEM((4 * ROWS, D), BF16),
            pltpu.VMEM((NC, NX, OWN, W), BF16),
            pltpu.VMEM((YLO, ROWS, NV), F32),
            pltpu.VMEM((YLO, ROWS, NV), BF16),
            pltpu.VMEM((2, NC, NX, OWN, W), BF16),
            pltpu.VMEM((2, NC, NX, OWN, W), BF16),
            pltpu.VMEM((2, NX, 1, ROWS), F32),
            pltpu.VMEM((ROWS, 128), F32),
            pltpu.VMEM((2, 2, NV), F32),
            pltpu.VMEM((NZ, 2, NV), F32),
            pltpu.VMEM((NY, 2, NV), F32),
            pltpu.VMEM((2, YLO, 2, NV), F32),
            pltpu.VMEM((2, NY, 2, 2, NV), F32),
            pltpu.VMEM((YLO, 2, NV), F32),
            pltpu.SemaphoreType.DMA((SEMS,)),
        ],
        compiler_params=pltpu.CompilerParams(
            collective_id=0, has_side_effects=True, vmem_limit_bytes=54272 * 2**10
        ),
    )(vectors, centroids)
    return result, log_norm.reshape(NV)


def solution(mesh):
    in_specs = (P("item", None), P("cent", None))
    out_specs = (P(("cent", "item"), None), P("item"))
    return jax.shard_map(shards, mesh=mesh, in_specs=in_specs, out_specs=out_specs, check_vma=False)
```

```python
import functools
import math

import jax
import jax.numpy as jnp
from jax import lax
from jax.experimental import pallas as pl
from jax.experimental.pallas import tpu as pltpu
from jax.sharding import PartitionSpec as P

MESH = pl.DeviceIdType.MESH
F32, BF16 = jnp.float32, jnp.bfloat16
BETA = 3.0
NX, NY, NZ, YLO = 4, 8, 8, 4
NV, D = 768, 1024
ROWS = 256
OWN = 64
NC = 4
W = D // NC
HALF = NV // 2
STEPS = 48, 32
PART, REST = 80, 32
GATHER = 2 * (3 * PART + 3 * REST + 3 * PART) + 3 * HALF
SEMS = 49
FARTHEST = (4, 3, 5, 2, 6, 1, 7)
SCALE = BETA / math.sqrt(D)


def nt(a, b):
    return lax.dot_general(a, b, (((1,), (1,)), ((), ())), preferred_element_type=F32)


def merge(pairs):
    peak = functools.reduce(jnp.maximum, [p for p, _ in pairs])
    return peak, sum(t * jnp.exp(p - peak) for p, t in pairs)


def local_stats(logits):
    peak = jnp.max(logits, axis=0, keepdims=True)
    return peak, jnp.sum(jnp.exp(logits - peak), axis=0, keepdims=True)


def half_sq(rows):
    wide = rows.astype(F32)
    return 0.5 * jnp.sum(wide * wide, axis=1, keepdims=True)


def kernel(
    vec, cen, out, logn,
    vall, cvm, cnew, lbuf, resp, wbuf, rbuf, mbuf, mcol,
    core1, zst1, yst1, core2, st2, fst2, sem, ready,
):
    item, cent = lax.axis_index("item"), lax.axis_index("cent")
    x, q = lax.rem(item, NX), item // NX
    z, yhi, c = cent // 4, lax.rem(cent // 2, 2), lax.rem(cent, 2)
    y = yhi * YLO + q
    names = {}

    def sem_of(name):
        return sem.at[names.setdefault(name, len(names))]

    ids = {}

    def dev(**to):
        if not all(isinstance(step, int) for step in to.values()):
            return dev_of(**to)
        key = tuple(to.items())
        if key not in ids:
            ids[key] = dev_of(**to)
        return ids[key]

    def dev_of(dx=0, dy=0, dz=0, dc=0):
        x2, y2 = lax.rem(x + dx + NX, NX), lax.rem(y + dy + NY, NY)
        z2, c2 = lax.rem(z + dz + NZ, NZ), lax.rem(c + dc, 2)
        return {"item": lax.rem(y2, YLO) * NX + x2, "cent": z2 * 4 + (y2 // YLO) * 2 + c2}

    def send(src, dst, group, arrived, **to):
        pltpu.make_async_remote_copy(
            src_ref=src, dst_ref=dst, send_sem=sem_of("s" + group), recv_sem=sem_of("r" + arrived),
            device_id=dev(**to), device_id_type=MESH,
        ).start()

    def wait(like, name):
        pltpu.make_async_copy(like, like, sem_of(name)).wait()

    barrier = pltpu.get_barrier_semaphore()
    around = [dict(dy=1), dict(dy=-1), dict(dz=1), dict(dz=-1), dict(dx=1), dict(dx=-1)]
    beyond = [dict(dy=2), dict(dy=-2), dict(dz=2), dict(dz=-2)]

    def tell(semaphore, peers):
        for to in peers:
            pl.semaphore_signal(semaphore, inc=1, device_id=dev(**to), device_id_type=MESH)

    tell(barrier, [dict(dc=1)] + around)
    mine = pl.ds(pl.multiple_of(q * NV, NV), NV)
    load_v = pltpu.make_async_copy(vec, vall.at[mine], sem_of("load_v"))
    load_c = pltpu.make_async_copy(cen, cvm, sem_of("load_c"))
    load_v.start()
    load_c.start()
    pl.semaphore_wait(barrier, 1 + len(around))
    tell(ready.at[0], around)

    par = lax.rem(z, 2)

    def rows_of(kind, high):
        if isinstance(kind, tuple):
            start, _ = rows_of(kind[0], high)
            return start + kind[1] * STEPS[0], STEPS[kind[1]]
        if kind == "rest":
            return c * HALF + 4 * PART + high * REST, REST
        share = par if kind == "own" else 1 - par
        return c * HALF + (2 * share + high) * PART, PART

    def piece(block, kind, high):
        start, n = rows_of(kind, high)
        b = lax.rem(q + block + YLO, YLO)
        return vall.at[pl.ds(pl.multiple_of(b * NV + start, 16), n)]

    def first(kind, high, arrived, **to):
        start, n = rows_of(kind, high)
        send(vec.at[pl.ds(pl.multiple_of(start, 16), n)], piece(0, kind, high), "gather", arrived, **to)

    def along(block, kind, high, arrived, **to):
        part = piece(block, kind, high)
        send(part, part, "gather", arrived, **to)

    def cross(block, kind, high):
        along(block, kind, high, "far" if block == 2 else "near", dc=1)

    def landed(n, name):
        wait(vall.at[pl.ds(0, n)], name)

    first("own", 0, "A", dy=1)
    first("own", 1, "A", dy=-1)
    first("own", 1, "B", dy=1)
    first("own", 0, "B", dy=-1)
    first("rest", 0, "C", dy=1)
    first("rest", 1, "C", dy=-1)
    load_v.wait()
    load_c.wait()

    def score(k, carry):
        rows = cvm[pl.ds(pl.multiple_of(k * ROWS, ROWS), ROWS), :]
        logits = SCALE * (nt(rows, vall[mine, :]) - half_sq(rows))
        lbuf[k] = logits
        return merge([carry, local_stats(logits)])

    carry = jnp.full((1, NV), -3.0e38, F32), jnp.zeros((1, NV), F32)
    carry = lax.fori_loop(0, 2, score, carry)
    pl.semaphore_wait(ready.at[0], len(around))
    tell(ready.at[1], beyond)
    peak, total = lax.fori_loop(2, 4, score, carry)
    core1[0, 0:1, :] = peak
    core1[0, 1:2, :] = total
    send(core1.at[0], core1.at[1], "core1", "core1", dc=1)
    wait(core1.at[1], "rcore1")
    peak, total = merge([(core1[k, 0:1, :], core1[k, 1:2, :]) for k in range(2)])
    zst1[z, 0:1, :] = peak
    zst1[z, 1:2, :] = total
    pl.semaphore_wait(ready.at[1], len(beyond))
    for k in FARTHEST:
        send(zst1.at[z], zst1.at[z], "zst", "zst", dz=k)

    landed(2 * PART, "rA")
    for h in range(2):
        along(-1, ("own", h), 0, f"F{h}", dy=1)
        along(1, ("own", h), 1, f"F{h}", dy=-1)
    along(-1, "own", 0, "Z0", dz=1)
    along(1, "own", 1, "Z0", dz=-1)
    first("rest", 1, "D", dy=1)
    first("rest", 0, "D", dy=-1)
    cross(-1, "own", 0)
    cross(1, "own", 1)
    landed(2 * PART, "rB")
    along(1, "own", 0, "Z1", dz=1)
    along(-1, "own", 1, "Z1", dz=-1)
    cross(-1, "own", 1)
    cross(1, "own", 0)

    wait(zst1.at[pl.ds(0, NZ - 1)], "rzst")
    peak, total = merge([(zst1[k, 0:1, :], zst1[k, 1:2, :]) for k in range(NZ)])
    yst1[y, 0:1, :] = peak
    yst1[y, 1:2, :] = total
    for k in FARTHEST:
        send(yst1.at[y], yst1.at[y], "yst", "yst", dy=k)

    for h in range(2):
        landed(2 * STEPS[h], f"rF{h}")
        along(2, ("own", h), 0, f"Y{h}", dz=1)
        along(2, ("own", h), 1, f"Y{h}", dz=-1)
    cross(2, "own", 0)
    cross(2, "own", 1)
    landed(2 * PART, "rZ0")
    cross(-1, "other", 0)
    cross(1, "other", 1)
    landed(2 * REST, "rC")
    along(-1, "rest", 0, "G", dy=1)
    along(1, "rest", 1, "G", dy=-1)
    cross(-1, "rest", 0)
    cross(1, "rest", 1)
    landed(2 * PART, "rZ1")
    cross(1, "other", 0)
    cross(-1, "other", 1)
    landed(2 * REST, "rD")
    cross(-1, "rest", 1)
    cross(1, "rest", 0)

    crow = pl.ds(pl.multiple_of(q * ROWS, ROWS), ROWS)
    half = half_sq(cvm[crow, :])

    def respond(block):
        b = lax.rem(q + block, YLO)
        peak, total = merge([(yst1[b + k, 0:1, :], yst1[b + k, 1:2, :]) for k in (0, YLO)])
        if block == 0:
            logits = lbuf[q]
        else:
            part = vall[pl.ds(pl.multiple_of(b * NV, NV), NV), :]
            logits = SCALE * (nt(cvm[crow, :], part) - half)
        resp[b] = (jnp.exp(logits - peak) * (1.0 / total)).astype(BF16)

    wait(yst1.at[pl.ds(0, NY - 1)], "ryst")
    respond(0)
    landed(2 * STEPS[0], "rY0")
    cross(2, ("other", 0), 0)
    cross(2, ("other", 0), 1)
    landed(2 * HALF, "rnear")
    respond(3)
    landed(2 * STEPS[1], "rY1")
    cross(2, ("other", 1), 0)
    cross(2, ("other", 1), 1)
    landed(2 * REST, "rG")
    cross(2, "rest", 0)
    cross(2, "rest", 1)
    respond(1)
    landed(HALF, "rfar")
    respond(2)

    own = pl.ds(pl.multiple_of(q * ROWS + x * OWN, OWN), OWN)
    own64 = pl.ds(pl.multiple_of(x * OWN, OWN), OWN)

    def reduce(it, old, emit):
        for n in range(NC):
            cols = slice(n * W, (n + 1) * W)
            part = sum(
                jnp.dot(resp[b], vall[b * NV : (b + 1) * NV, cols], preferred_element_type=F32)
                for b in range(YLO)
            )
            wbuf[it, n] = part.astype(BF16).reshape(NX, OWN, W)
            rbuf[it, n, 0] = wbuf[it, n, x]
            for k in (2, 1, 3):
                send(
                    wbuf.at[it, n, lax.rem(x + k, NX)], rbuf.at[it, n, k],
                    f"rs{it}", f"rs{it}{n}", dx=k,
                )
            if n == 0:
                mass = sum(jnp.sum(resp[b].astype(F32), axis=1, keepdims=True) for b in range(YLO))
                mbuf[it, x] = jnp.transpose(jnp.broadcast_to(mass, (ROWS, 128)))[0:1, :]
                for k in range(1, NX):
                    send(mbuf.at[it, x], mbuf.at[it, x], f"m{it}", f"m{it}", dx=k)
        wait(mbuf.at[it, pl.ds(0, NX - 1)], f"rm{it}")
        row = sum(mbuf[it, k] for k in range(NX))
        mcol[...] = jnp.transpose(jnp.broadcast_to(row, (128, ROWS)))
        div = mcol[own64, 0:1] + 1.0
        for n in range(NC):
            wait(rbuf.at[it, n, pl.ds(1, NX - 1)], f"rrs{it}{n}")
            sums = sum(rbuf[it, n, k].astype(F32) for k in range(NX))
            emit(n, ((sums + old(n).astype(F32)) / div).astype(BF16))

    def spread(n, fresh):
        cnew[n, x] = fresh
        for k in (2, 1, 3):
            send(cnew.at[n, x], cnew.at[n, x], "ag", f"ag{n}", dx=k)

    reduce(0, lambda n: cvm[own, n * W : (n + 1) * W], spread)

    half = jnp.zeros((ROWS, 1), F32)
    for n in range(NC):
        wait(cnew.at[n, pl.ds(0, NX - 1)], f"rag{n}")
        rows = cnew[n].reshape(ROWS, W)
        half = half + half_sq(rows)
        for b in range(YLO):
            term = nt(rows, vall[b * NV : (b + 1) * NV, n * W : (n + 1) * W])
            if n > 0:
                term = lbuf[b] + term
            if n < NC - 1:
                lbuf[b] = term
            else:
                logits = SCALE * (term - half)
                peak = jnp.max(logits, axis=0, keepdims=True)
                expo = jnp.exp(logits - peak)
                lbuf[b] = expo
                core2[0, b, 0:1, :] = peak
                core2[0, b, 1:2, :] = jnp.sum(expo, axis=0, keepdims=True)

    theirs = pl.ds(2 - 2 * c, 2)
    pair = pl.ds(2 * c, 2)
    send(core2.at[0, theirs], core2.at[1, theirs], "core2", "core2", dc=1)
    wait(core2.at[1, pair], "rcore2")
    found = [
        merge([(core2[k, 2 * c + j, 0:1, :], core2[k, 2 * c + j, 1:2, :]) for k in range(2)]) for j in range(2)
    ]
    for s in range(2):
        turn = lax.rem(c + s, 2)
        at = y * (1 - turn) + z * turn
        for j in range(2):
            st2[s, at, j, 0:1, :], st2[s, at, j, 1:2, :] = found[j]
        for k in FARTHEST:
            send(st2.at[s, at], st2.at[s, at], f"st{s}", f"st{s}", dy=k * (1 - turn), dz=k * turn)
        wait(st2.at[s, pl.ds(0, NY - 1)], f"rst{s}")
        found = [merge([(st2[s, k, j, 0:1, :], st2[s, k, j, 1:2, :]) for k in range(NY)]) for j in range(2)]
    for j in range(2):
        fst2[2 * c + j, 0:1, :], fst2[2 * c + j, 1:2, :] = found[j]
    send(fst2.at[pair], fst2.at[pair], "core3", "core3", dc=1)
    wait(fst2.at[theirs], "rcore3")

    for b in range(YLO):
        peak, total = fst2[b, 0:1, :], fst2[b, 1:2, :]
        share = jnp.exp(core2[0, b, 0:1, :] - peak) * (1.0 / total)
        resp[b] = (lbuf[b] * share).astype(BF16)

    def finish(n, fresh):
        out[:, n * W : (n + 1) * W] = fresh

    reduce(1, lambda n: cnew[n, x], finish)
    norm = fst2[q, 0:1, :] + jnp.log(fst2[q, 1:2, :])
    for k in range(NV // 128):
        logn[k : k + 1, :] = norm[:, k * 128 : (k + 1) * 128]

    landed(GATHER, "sgather")
    wait(core1.at[0], "score1")
    wait(zst1.at[pl.ds(0, NZ - 1)], "szst")
    wait(yst1.at[pl.ds(0, NY - 1)], "syst")
    for it in range(2):
        wait(rbuf.at[it, pl.ds(0, NX - 1)], f"srs{it}")
        wait(mbuf.at[it, pl.ds(0, NX - 1)], f"sm{it}")
        wait(st2.at[it, pl.ds(0, NY - 1)], f"sst{it}")
    wait(cnew.at[pl.ds(0, NX - 1)], "sag")
    wait(core2.at[0, pair], "score2")
    wait(fst2.at[pair], "score3")
    assert len(names) == SEMS, len(names)


def shards(vectors, centroids):
    result, log_norm = pl.pallas_call(
        kernel,
        out_shape=(
            jax.ShapeDtypeStruct((OWN, D), BF16),
            jax.ShapeDtypeStruct((NV // 128, 128), F32),
        ),
        in_specs=[pl.BlockSpec(memory_space=pl.ANY)] * 2,
        out_specs=(pl.BlockSpec(memory_space=pltpu.VMEM),) * 2,
        scratch_shapes=[
            pltpu.VMEM((YLO * NV, D), BF16),
            pltpu.VMEM((4 * ROWS, D), BF16),
            pltpu.VMEM((NC, NX, OWN, W), BF16),
            pltpu.VMEM((YLO, ROWS, NV), F32),
            pltpu.VMEM((YLO, ROWS, NV), BF16),
            pltpu.VMEM((2, NC, NX, OWN, W), BF16),
            pltpu.VMEM((2, NC, NX, OWN, W), BF16),
            pltpu.VMEM((2, NX, 1, ROWS), F32),
            pltpu.VMEM((ROWS, 128), F32),
            pltpu.VMEM((2, 2, NV), F32),
            pltpu.VMEM((NZ, 2, NV), F32),
            pltpu.VMEM((NY, 2, NV), F32),
            pltpu.VMEM((2, YLO, 2, NV), F32),
            pltpu.VMEM((2, NY, 2, 2, NV), F32),
            pltpu.VMEM((YLO, 2, NV), F32),
            pltpu.SemaphoreType.DMA((SEMS,)),
            pltpu.SemaphoreType.REGULAR((2,)),
        ],
        compiler_params=pltpu.CompilerParams(
            collective_id=0, has_side_effects=True, vmem_limit_bytes=54272 * 2**10
        ),
    )(vectors, centroids)
    return result, log_norm.reshape(NV)


def solution(mesh):
    in_specs = (P("item", None), P("cent", None))
    out_specs = (P(("cent", "item"), None), P("item"))
    return jax.shard_map(shards, mesh=mesh, in_specs=in_specs, out_specs=out_specs, check_vma=False)
```

```python
import functools
import math

import jax
import jax.numpy as jnp
from jax import lax
from jax.experimental import pallas as pl
from jax.experimental.pallas import tpu as pltpu
from jax.sharding import PartitionSpec as P

MESH = pl.DeviceIdType.MESH
F32, BF16 = jnp.float32, jnp.bfloat16
BETA = 3.0
NX, NY, NZ, YLO = 4, 8, 8, 4
NV, D = 768, 1024
ROWS = 256
OWN = 64
NC = 4
W = D // NC
HALF = NV // 2
STEPS = 48, 32
PART, REST = 80, 32
GATHER = 2 * (3 * PART + 3 * REST + 3 * PART) + 3 * HALF
SEMS = 49
FARTHEST = (4, 3, 5, 2, 6, 1, 7)
SCALE = BETA / math.sqrt(D)


def nt(a, b):
    return lax.dot_general(a, b, (((1,), (1,)), ((), ())), preferred_element_type=F32)


def merge(pairs):
    peak = functools.reduce(jnp.maximum, [p for p, _ in pairs])
    return peak, sum(t * jnp.exp(p - peak) for p, t in pairs)


def local_stats(logits):
    peak = jnp.max(logits, axis=0, keepdims=True)
    return peak, jnp.sum(jnp.exp(logits - peak), axis=0, keepdims=True)


def half_sq(rows):
    wide = rows.astype(F32)
    return 0.5 * jnp.sum(wide * wide, axis=1, keepdims=True)


def kernel(
    vec, cen, out, logn,
    vall, cvm, cnew, lbuf, resp, wbuf, rbuf, mbuf, mcol,
    core1, zst1, yst1, core2, st2, fst2, sem, ready,
):
    item, cent = lax.axis_index("item"), lax.axis_index("cent")
    x, q = lax.rem(item, NX), item // NX
    z, yhi, c = cent // 4, lax.rem(cent // 2, 2), lax.rem(cent, 2)
    y = yhi * YLO + q
    names = {}

    def sem_of(name):
        return sem.at[names.setdefault(name, len(names))]

    ids = {}

    def dev(**to):
        if not all(isinstance(step, int) for step in to.values()):
            return dev_of(**to)
        key = tuple(to.items())
        if key not in ids:
            ids[key] = dev_of(**to)
        return ids[key]

    def dev_of(dx=0, dy=0, dz=0, dc=0):
        x2, y2 = lax.rem(x + dx + NX, NX), lax.rem(y + dy + NY, NY)
        z2, c2 = lax.rem(z + dz + NZ, NZ), lax.rem(c + dc, 2)
        return {"item": lax.rem(y2, YLO) * NX + x2, "cent": z2 * 4 + (y2 // YLO) * 2 + c2}

    def send(src, dst, group, arrived, **to):
        pltpu.make_async_remote_copy(
            src_ref=src, dst_ref=dst, send_sem=sem_of("s" + group), recv_sem=sem_of("r" + arrived),
            device_id=dev(**to), device_id_type=MESH,
        ).start()

    def wait(like, name):
        pltpu.make_async_copy(like, like, sem_of(name)).wait()

    barrier = pltpu.get_barrier_semaphore()
    around = [dict(dy=1), dict(dy=-1), dict(dz=1), dict(dz=-1), dict(dx=1), dict(dx=-1)]
    beyond = [dict(dy=2), dict(dy=-2), dict(dz=2), dict(dz=-2)]

    def tell(semaphore, peers):
        for to in peers:
            pl.semaphore_signal(semaphore, inc=1, device_id=dev(**to), device_id_type=MESH)

    tell(barrier, [dict(dc=1)] + around)
    mine = pl.ds(pl.multiple_of(q * NV, NV), NV)
    load_v = pltpu.make_async_copy(vec, vall.at[mine], sem_of("load_v"))
    load_c = pltpu.make_async_copy(cen, cvm, sem_of("load_c"))
    load_v.start()
    load_c.start()
    pl.semaphore_wait(barrier, 1 + len(around))
    tell(ready.at[0], around)

    par = lax.rem(z, 2)

    def rows_of(kind, high):
        if isinstance(kind, tuple):
            start, _ = rows_of(kind[0], high)
            return start + kind[1] * STEPS[0], STEPS[kind[1]]
        if kind == "rest":
            return c * HALF + 4 * PART + high * REST, REST
        share = par if kind == "own" else 1 - par
        return c * HALF + (2 * share + high) * PART, PART

    def piece(block, kind, high):
        start, n = rows_of(kind, high)
        b = lax.rem(q + block + YLO, YLO)
        return vall.at[pl.ds(pl.multiple_of(b * NV + start, 16), n)]

    def first(kind, high, arrived, **to):
        start, n = rows_of(kind, high)
        send(vec.at[pl.ds(pl.multiple_of(start, 16), n)], piece(0, kind, high), "gather", arrived, **to)

    def along(block, kind, high, arrived, **to):
        part = piece(block, kind, high)
        send(part, part, "gather", arrived, **to)

    def cross(block, kind, high):
        along(block, kind, high, "far" if block == 2 else "near", dc=1)

    def landed(n, name):
        wait(vall.at[pl.ds(0, n)], name)

    first("own", 0, "A", dy=1)
    first("own", 1, "A", dy=-1)
    first("own", 1, "B", dy=1)
    first("own", 0, "B", dy=-1)
    first("rest", 0, "C", dy=1)
    first("rest", 1, "C", dy=-1)
    load_v.wait()
    load_c.wait()

    def score(k, carry):
        rows = cvm[pl.ds(pl.multiple_of(k * ROWS, ROWS), ROWS), :]
        logits = SCALE * (nt(rows, vall[mine, :]) - half_sq(rows))
        lbuf[k] = logits
        return merge([carry, local_stats(logits)])

    carry = jnp.full((1, NV), -3.0e38, F32), jnp.zeros((1, NV), F32)
    carry = lax.fori_loop(0, 2, score, carry)
    pl.semaphore_wait(ready.at[0], len(around))
    tell(ready.at[1], beyond)
    peak, total = lax.fori_loop(2, 4, score, carry)
    core1[0, 0:1, :] = peak
    core1[0, 1:2, :] = total
    send(core1.at[0], core1.at[1], "core1", "core1", dc=1)
    wait(core1.at[1], "rcore1")
    peak, total = merge([(core1[k, 0:1, :], core1[k, 1:2, :]) for k in range(2)])
    zst1[z, 0:1, :] = peak
    zst1[z, 1:2, :] = total
    pl.semaphore_wait(ready.at[1], len(beyond))
    for k in FARTHEST:
        send(zst1.at[z], zst1.at[z], "zst", "zst", dz=k)

    landed(2 * PART, "rA")
    for h in range(2):
        along(-1, ("own", h), 0, f"F{h}", dy=1)
        along(1, ("own", h), 1, f"F{h}", dy=-1)
    along(-1, "own", 0, "Z0", dz=1)
    along(1, "own", 1, "Z0", dz=-1)
    first("rest", 1, "D", dy=1)
    first("rest", 0, "D", dy=-1)
    cross(-1, "own", 0)
    cross(1, "own", 1)
    landed(2 * PART, "rB")
    along(1, "own", 0, "Z1", dz=1)
    along(-1, "own", 1, "Z1", dz=-1)
    cross(-1, "own", 1)
    cross(1, "own", 0)

    wait(zst1.at[pl.ds(0, NZ - 1)], "rzst")
    peak, total = merge([(zst1[k, 0:1, :], zst1[k, 1:2, :]) for k in range(NZ)])
    yst1[y, 0:1, :] = peak
    yst1[y, 1:2, :] = total
    for k in FARTHEST:
        send(yst1.at[y], yst1.at[y], "yst", "yst", dy=k)

    for h in range(2):
        landed(2 * STEPS[h], f"rF{h}")
        along(2, ("own", h), 0, f"Y{h}", dz=1)
        along(2, ("own", h), 1, f"Y{h}", dz=-1)
    cross(2, "own", 0)
    cross(2, "own", 1)
    landed(2 * PART, "rZ0")
    cross(-1, "other", 0)
    cross(1, "other", 1)
    landed(2 * REST, "rC")
    along(-1, "rest", 0, "G", dy=1)
    along(1, "rest", 1, "G", dy=-1)
    cross(-1, "rest", 0)
    cross(1, "rest", 1)
    landed(2 * PART, "rZ1")
    cross(1, "other", 0)
    cross(-1, "other", 1)
    landed(2 * REST, "rD")
    cross(-1, "rest", 1)
    cross(1, "rest", 0)

    crow = pl.ds(pl.multiple_of(q * ROWS, ROWS), ROWS)
    half = half_sq(cvm[crow, :])

    def respond(block):
        b = lax.rem(q + block, YLO)
        peak, total = merge([(yst1[b + k, 0:1, :], yst1[b + k, 1:2, :]) for k in (0, YLO)])
        if block == 0:
            logits = lbuf[q]
        else:
            part = vall[pl.ds(pl.multiple_of(b * NV, NV), NV), :]
            logits = SCALE * (nt(cvm[crow, :], part) - half)
        resp[b] = (jnp.exp(logits - peak) * (1.0 / total)).astype(BF16)

    wait(yst1.at[pl.ds(0, NY - 1)], "ryst")
    respond(0)
    landed(2 * STEPS[0], "rY0")
    cross(2, ("other", 0), 0)
    cross(2, ("other", 0), 1)
    landed(2 * HALF, "rnear")
    respond(3)
    landed(2 * STEPS[1], "rY1")
    cross(2, ("other", 1), 0)
    cross(2, ("other", 1), 1)
    landed(2 * REST, "rG")
    cross(2, "rest", 0)
    cross(2, "rest", 1)
    respond(1)
    landed(HALF, "rfar")
    respond(2)

    own = pl.ds(pl.multiple_of(q * ROWS + x * OWN, OWN), OWN)
    own64 = pl.ds(pl.multiple_of(x * OWN, OWN), OWN)

    def reduce(it, old, emit):
        for n in range(NC):
            cols = slice(n * W, (n + 1) * W)
            part = sum(
                jnp.dot(resp[b], vall[b * NV : (b + 1) * NV, cols], preferred_element_type=F32)
                for b in range(YLO)
            )
            wbuf[it, n] = part.astype(BF16).reshape(NX, OWN, W)
            rbuf[it, n, 0] = wbuf[it, n, x]
            for k in (2, 1, 3):
                send(
                    wbuf.at[it, n, lax.rem(x + k, NX)], rbuf.at[it, n, k],
                    f"rs{it}", f"rs{it}{n}", dx=k,
                )
            if n == 0:
                mass = sum(jnp.sum(resp[b].astype(F32), axis=1, keepdims=True) for b in range(YLO))
                mbuf[it, x] = jnp.transpose(jnp.broadcast_to(mass, (ROWS, 128)))[0:1, :]
                for k in range(1, NX):
                    send(mbuf.at[it, x], mbuf.at[it, x], f"m{it}", f"m{it}", dx=k)
        wait(mbuf.at[it, pl.ds(0, NX - 1)], f"rm{it}")
        row = sum(mbuf[it, k] for k in range(NX))
        mcol[...] = jnp.transpose(jnp.broadcast_to(row, (128, ROWS)))
        div = mcol[own64, 0:1] + 1.0
        for n in range(NC):
            wait(rbuf.at[it, n, pl.ds(1, NX - 1)], f"rrs{it}{n}")
            sums = sum(rbuf[it, n, k].astype(F32) for k in range(NX))
            emit(n, ((sums + old(n).astype(F32)) / div).astype(BF16))

    def spread(n, fresh):
        cnew[n, x] = fresh
        for k in (2, 1, 3):
            send(cnew.at[n, x], cnew.at[n, x], "ag", f"ag{n}", dx=k)

    reduce(0, lambda n: cvm[own, n * W : (n + 1) * W], spread)

    half = jnp.zeros((ROWS, 1), F32)
    theirs = pl.ds(2 - 2 * c, 2)
    pair = pl.ds(2 * c, 2)
    for n in range(NC):
        wait(cnew.at[n, pl.ds(0, NX - 1)], f"rag{n}")
        rows = cnew[n].reshape(ROWS, W)
        half = half + half_sq(rows)
        for i in range(YLO):
            b = i if n < NC - 1 else lax.rem(2 - 2 * c + i, YLO)
            start = b * NV if n < NC - 1 else pl.multiple_of(b * NV, NV)
            term = nt(rows, vall[pl.ds(start, NV), n * W : (n + 1) * W])
            if n > 0:
                term = lbuf[b] + term
            if n < NC - 1:
                lbuf[b] = term
            else:
                logits = SCALE * (term - half)
                peak = jnp.max(logits, axis=0, keepdims=True)
                expo = jnp.exp(logits - peak)
                lbuf[b] = expo
                core2[0, b, 0:1, :] = peak
                core2[0, b, 1:2, :] = jnp.sum(expo, axis=0, keepdims=True)
                if i == 1:
                    send(core2.at[0, theirs], core2.at[1, theirs], "core2", "core2", dc=1)

    wait(core2.at[1, pair], "rcore2")
    found = [
        merge([(core2[k, 2 * c + j, 0:1, :], core2[k, 2 * c + j, 1:2, :]) for k in range(2)]) for j in range(2)
    ]
    for s in range(2):
        turn = lax.rem(c + s, 2)
        at = y * (1 - turn) + z * turn
        for j in range(2):
            st2[s, at, j, 0:1, :], st2[s, at, j, 1:2, :] = found[j]
        for k in FARTHEST:
            send(st2.at[s, at], st2.at[s, at], f"st{s}", f"st{s}", dy=k * (1 - turn), dz=k * turn)
        wait(st2.at[s, pl.ds(0, NY - 1)], f"rst{s}")
        found = [merge([(st2[s, k, j, 0:1, :], st2[s, k, j, 1:2, :]) for k in range(NY)]) for j in range(2)]
    for j in range(2):
        fst2[2 * c + j, 0:1, :], fst2[2 * c + j, 1:2, :] = found[j]
    send(fst2.at[pair], fst2.at[pair], "core3", "core3", dc=1)

    for i in range(YLO):
        if i == 2:
            wait(fst2.at[theirs], "rcore3")
        b = lax.rem(2 * c + i, YLO)
        peak, total = fst2[b, 0:1, :], fst2[b, 1:2, :]
        share = jnp.exp(core2[0, b, 0:1, :] - peak) * (1.0 / total)
        resp[b] = (lbuf[b] * share).astype(BF16)

    def finish(n, fresh):
        out[:, n * W : (n + 1) * W] = fresh

    reduce(1, lambda n: cnew[n, x], finish)
    norm = fst2[q, 0:1, :] + jnp.log(fst2[q, 1:2, :])
    for k in range(NV // 128):
        logn[k : k + 1, :] = norm[:, k * 128 : (k + 1) * 128]

    landed(GATHER, "sgather")
    wait(core1.at[0], "score1")
    wait(zst1.at[pl.ds(0, NZ - 1)], "szst")
    wait(yst1.at[pl.ds(0, NY - 1)], "syst")
    for it in range(2):
        wait(rbuf.at[it, pl.ds(0, NX - 1)], f"srs{it}")
        wait(mbuf.at[it, pl.ds(0, NX - 1)], f"sm{it}")
        wait(st2.at[it, pl.ds(0, NY - 1)], f"sst{it}")
    wait(cnew.at[pl.ds(0, NX - 1)], "sag")
    wait(core2.at[0, pair], "score2")
    wait(fst2.at[pair], "score3")
    assert len(names) == SEMS, len(names)


def shards(vectors, centroids):
    result, log_norm = pl.pallas_call(
        kernel,
        out_shape=(
            jax.ShapeDtypeStruct((OWN, D), BF16),
            jax.ShapeDtypeStruct((NV // 128, 128), F32),
        ),
        in_specs=[pl.BlockSpec(memory_space=pl.ANY)] * 2,
        out_specs=(pl.BlockSpec(memory_space=pltpu.VMEM),) * 2,
        scratch_shapes=[
            pltpu.VMEM((YLO * NV, D), BF16),
            pltpu.VMEM((4 * ROWS, D), BF16),
            pltpu.VMEM((NC, NX, OWN, W), BF16),
            pltpu.VMEM((YLO, ROWS, NV), F32),
            pltpu.VMEM((YLO, ROWS, NV), BF16),
            pltpu.VMEM((2, NC, NX, OWN, W), BF16),
            pltpu.VMEM((2, NC, NX, OWN, W), BF16),
            pltpu.VMEM((2, NX, 1, ROWS), F32),
            pltpu.VMEM((ROWS, 128), F32),
            pltpu.VMEM((2, 2, NV), F32),
            pltpu.VMEM((NZ, 2, NV), F32),
            pltpu.VMEM((NY, 2, NV), F32),
            pltpu.VMEM((2, YLO, 2, NV), F32),
            pltpu.VMEM((2, NY, 2, 2, NV), F32),
            pltpu.VMEM((YLO, 2, NV), F32),
            pltpu.SemaphoreType.DMA((SEMS,)),
            pltpu.SemaphoreType.REGULAR((2,)),
        ],
        compiler_params=pltpu.CompilerParams(
            collective_id=0, has_side_effects=True, vmem_limit_bytes=54272 * 2**10
        ),
    )(vectors, centroids)
    return result, log_norm.reshape(NV)


def solution(mesh):
    in_specs = (P("item", None), P("cent", None))
    out_specs = (P(("cent", "item"), None), P("item"))
    return jax.shard_map(shards, mesh=mesh, in_specs=in_specs, out_specs=out_specs, check_vma=False)
```

```python
import functools
import math

import jax
import jax.numpy as jnp
from jax import lax
from jax.experimental import pallas as pl
from jax.experimental.pallas import tpu as pltpu
from jax.sharding import PartitionSpec as P

MESH = pl.DeviceIdType.MESH
F32, BF16 = jnp.float32, jnp.bfloat16
BETA = 3.0
NX, NY, NZ, YLO = 4, 8, 8, 4
NV, D = 768, 1024
ROWS = 256
OWN = 64
NC = 4
W = D // NC
HALF = NV // 2
STEPS = 48, 32
PART, REST = 80, 32
GATHER = 2 * (3 * PART + 3 * REST + 3 * PART) + 3 * HALF
SEMS = 49
FARTHEST = (4, 3, 5, 2, 6, 1, 7)
SCALE = BETA / math.sqrt(D)


def nt(a, b):
    return lax.dot_general(a, b, (((1,), (1,)), ((), ())), preferred_element_type=F32)


def merge(pairs):
    peak = functools.reduce(jnp.maximum, [p for p, _ in pairs])
    return peak, sum(t * jnp.exp(p - peak) for p, t in pairs)


def rows_at(b):
    start = b * NV
    return pl.ds(start if isinstance(b, int) else pl.multiple_of(start, NV), NV)


def local_stats(logits):
    peak = jnp.max(logits, axis=0, keepdims=True)
    return peak, jnp.sum(jnp.exp(logits - peak), axis=0, keepdims=True)


def half_sq(rows):
    wide = rows.astype(F32)
    return 0.5 * jnp.sum(wide * wide, axis=1, keepdims=True)


def kernel(
    vec, cen, out, logn,
    vall, cvm, cnew, lbuf, resp, acc, wbuf, rbuf, mbuf, mcol,
    core1, zst1, yst1, core2, st2, fst2, sem, ready,
):
    item, cent = lax.axis_index("item"), lax.axis_index("cent")
    x, q = lax.rem(item, NX), item // NX
    z, yhi, c = cent // 4, lax.rem(cent // 2, 2), lax.rem(cent, 2)
    y = yhi * YLO + q
    names = {}

    def sem_of(name):
        return sem.at[names.setdefault(name, len(names))]

    ids = {}

    def dev(**to):
        if not all(isinstance(step, int) for step in to.values()):
            return dev_of(**to)
        key = tuple(to.items())
        if key not in ids:
            ids[key] = dev_of(**to)
        return ids[key]

    def dev_of(dx=0, dy=0, dz=0, dc=0):
        x2, y2 = lax.rem(x + dx + NX, NX), lax.rem(y + dy + NY, NY)
        z2, c2 = lax.rem(z + dz + NZ, NZ), lax.rem(c + dc, 2)
        return {"item": lax.rem(y2, YLO) * NX + x2, "cent": z2 * 4 + (y2 // YLO) * 2 + c2}

    def send(src, dst, group, arrived, **to):
        pltpu.make_async_remote_copy(
            src_ref=src, dst_ref=dst, send_sem=sem_of("s" + group), recv_sem=sem_of("r" + arrived),
            device_id=dev(**to), device_id_type=MESH,
        ).start()

    def wait(like, name):
        pltpu.make_async_copy(like, like, sem_of(name)).wait()

    barrier = pltpu.get_barrier_semaphore()
    around = [dict(dy=1), dict(dy=-1), dict(dz=1), dict(dz=-1), dict(dx=1), dict(dx=-1)]
    beyond = [dict(dy=2), dict(dy=-2), dict(dz=2), dict(dz=-2)]

    def tell(semaphore, peers):
        for to in peers:
            pl.semaphore_signal(semaphore, inc=1, device_id=dev(**to), device_id_type=MESH)

    tell(barrier, [dict(dc=1)] + around)
    mine = pl.ds(pl.multiple_of(q * NV, NV), NV)
    load_v = pltpu.make_async_copy(vec, vall.at[mine], sem_of("load_v"))
    load_c = pltpu.make_async_copy(cen, cvm, sem_of("load_c"))
    load_v.start()
    load_c.start()
    pl.semaphore_wait(barrier, 1 + len(around))
    tell(ready.at[0], around)

    par = lax.rem(z, 2)

    def rows_of(kind, high):
        if isinstance(kind, tuple):
            start, _ = rows_of(kind[0], high)
            return start + kind[1] * STEPS[0], STEPS[kind[1]]
        if kind == "rest":
            return c * HALF + 4 * PART + high * REST, REST
        share = par if kind == "own" else 1 - par
        return c * HALF + (2 * share + high) * PART, PART

    def piece(block, kind, high):
        start, n = rows_of(kind, high)
        b = lax.rem(q + block + YLO, YLO)
        return vall.at[pl.ds(pl.multiple_of(b * NV + start, 16), n)]

    def first(kind, high, arrived, **to):
        start, n = rows_of(kind, high)
        send(vec.at[pl.ds(pl.multiple_of(start, 16), n)], piece(0, kind, high), "gather", arrived, **to)

    def along(block, kind, high, arrived, **to):
        part = piece(block, kind, high)
        send(part, part, "gather", arrived, **to)

    def cross(block, kind, high):
        along(block, kind, high, "far" if block == 2 else "near", dc=1)

    def landed(n, name):
        wait(vall.at[pl.ds(0, n)], name)

    first("own", 0, "A", dy=1)
    first("own", 1, "A", dy=-1)
    first("own", 1, "B", dy=1)
    first("own", 0, "B", dy=-1)
    first("rest", 0, "C", dy=1)
    first("rest", 1, "C", dy=-1)
    load_v.wait()
    load_c.wait()

    def score(k, carry):
        rows = cvm[pl.ds(pl.multiple_of(k * ROWS, ROWS), ROWS), :]
        logits = SCALE * (nt(rows, vall[mine, :]) - half_sq(rows))
        lbuf[k] = logits
        return merge([carry, local_stats(logits)])

    carry = jnp.full((1, NV), -3.0e38, F32), jnp.zeros((1, NV), F32)
    carry = lax.fori_loop(0, 2, score, carry)
    pl.semaphore_wait(ready.at[0], len(around))
    tell(ready.at[1], beyond)
    peak, total = lax.fori_loop(2, 4, score, carry)
    core1[0, 0:1, :] = peak
    core1[0, 1:2, :] = total
    send(core1.at[0], core1.at[1], "core1", "core1", dc=1)
    wait(core1.at[1], "rcore1")
    peak, total = merge([(core1[k, 0:1, :], core1[k, 1:2, :]) for k in range(2)])
    zst1[z, 0:1, :] = peak
    zst1[z, 1:2, :] = total
    pl.semaphore_wait(ready.at[1], len(beyond))
    for k in FARTHEST:
        send(zst1.at[z], zst1.at[z], "zst", "zst", dz=k)

    landed(2 * PART, "rA")
    for h in range(2):
        along(-1, ("own", h), 0, f"F{h}", dy=1)
        along(1, ("own", h), 1, f"F{h}", dy=-1)
    along(-1, "own", 0, "Z0", dz=1)
    along(1, "own", 1, "Z0", dz=-1)
    first("rest", 1, "D", dy=1)
    first("rest", 0, "D", dy=-1)
    cross(-1, "own", 0)
    cross(1, "own", 1)
    landed(2 * PART, "rB")
    along(1, "own", 0, "Z1", dz=1)
    along(-1, "own", 1, "Z1", dz=-1)
    cross(-1, "own", 1)
    cross(1, "own", 0)

    wait(zst1.at[pl.ds(0, NZ - 1)], "rzst")
    peak, total = merge([(zst1[k, 0:1, :], zst1[k, 1:2, :]) for k in range(NZ)])
    yst1[y, 0:1, :] = peak
    yst1[y, 1:2, :] = total
    for k in FARTHEST:
        send(yst1.at[y], yst1.at[y], "yst", "yst", dy=k)

    for h in range(2):
        landed(2 * STEPS[h], f"rF{h}")
        along(2, ("own", h), 0, f"Y{h}", dz=1)
        along(2, ("own", h), 1, f"Y{h}", dz=-1)
    cross(2, "own", 0)
    cross(2, "own", 1)
    landed(2 * PART, "rZ0")
    cross(-1, "other", 0)
    cross(1, "other", 1)
    landed(2 * REST, "rC")
    along(-1, "rest", 0, "G", dy=1)
    along(1, "rest", 1, "G", dy=-1)
    cross(-1, "rest", 0)
    cross(1, "rest", 1)
    landed(2 * PART, "rZ1")
    cross(1, "other", 0)
    cross(-1, "other", 1)
    landed(2 * REST, "rD")
    cross(-1, "rest", 1)
    cross(1, "rest", 0)

    crow = pl.ds(pl.multiple_of(q * ROWS, ROWS), ROWS)
    half = half_sq(cvm[crow, :])

    def respond(block):
        b = lax.rem(q + block, YLO)
        peak, total = merge([(yst1[b + k, 0:1, :], yst1[b + k, 1:2, :]) for k in (0, YLO)])
        if block == 0:
            logits = lbuf[q]
        else:
            part = vall[pl.ds(pl.multiple_of(b * NV, NV), NV), :]
            logits = SCALE * (nt(cvm[crow, :], part) - half)
        resp[b] = (jnp.exp(logits - peak) * (1.0 / total)).astype(BF16)

    wait(yst1.at[pl.ds(0, NY - 1)], "ryst")
    respond(0)
    landed(2 * STEPS[0], "rY0")
    cross(2, ("other", 0), 0)
    cross(2, ("other", 0), 1)
    landed(2 * HALF, "rnear")
    respond(3)
    landed(2 * STEPS[1], "rY1")
    cross(2, ("other", 1), 0)
    cross(2, ("other", 1), 1)
    landed(2 * REST, "rG")
    cross(2, "rest", 0)
    cross(2, "rest", 1)
    respond(1)

    def weigh(b, n):
        part = vall[rows_at(b), n * W : (n + 1) * W]
        return jnp.dot(resp[b], part, preferred_element_type=F32)

    acc[...] = sum(weigh(lax.rem(q + k, YLO), 0) for k in (0, 3, 1))
    landed(HALF, "rfar")
    respond(2)

    own = pl.ds(pl.multiple_of(q * ROWS + x * OWN, OWN), OWN)
    own64 = pl.ds(pl.multiple_of(x * OWN, OWN), OWN)

    def reduce(it, late, old, emit):
        for n in range(NC):
            if n == 0:
                part = acc[...] + sum(weigh(b, 0) for b in late)
            else:
                part = sum(weigh(b, n) for b in range(YLO))
            wbuf[it, n] = part.astype(BF16).reshape(NX, OWN, W)
            rbuf[it, n, 0] = wbuf[it, n, x]
            for k in (2, 1, 3):
                send(
                    wbuf.at[it, n, lax.rem(x + k, NX)], rbuf.at[it, n, k],
                    f"rs{it}", f"rs{it}{n}", dx=k,
                )
            if n == 0:
                mass = sum(jnp.sum(resp[b].astype(F32), axis=1, keepdims=True) for b in range(YLO))
                mbuf[it, x] = jnp.transpose(jnp.broadcast_to(mass, (ROWS, 128)))[0:1, :]
                for k in range(1, NX):
                    send(mbuf.at[it, x], mbuf.at[it, x], f"m{it}", f"m{it}", dx=k)
        wait(mbuf.at[it, pl.ds(0, NX - 1)], f"rm{it}")
        row = sum(mbuf[it, k] for k in range(NX))
        mcol[...] = jnp.transpose(jnp.broadcast_to(row, (128, ROWS)))
        div = mcol[own64, 0:1] + 1.0
        for n in range(NC):
            wait(rbuf.at[it, n, pl.ds(1, NX - 1)], f"rrs{it}{n}")
            sums = sum(rbuf[it, n, k].astype(F32) for k in range(NX))
            emit(n, ((sums + old(n).astype(F32)) / div).astype(BF16))

    def spread(n, fresh):
        cnew[n, x] = fresh
        for k in (2, 1, 3):
            send(cnew.at[n, x], cnew.at[n, x], "ag", f"ag{n}", dx=k)

    reduce(0, [lax.rem(q + 2, YLO)], lambda n: cvm[own, n * W : (n + 1) * W], spread)

    half = jnp.zeros((ROWS, 1), F32)
    theirs = pl.ds(2 - 2 * c, 2)
    pair = pl.ds(2 * c, 2)
    for n in range(NC):
        wait(cnew.at[n, pl.ds(0, NX - 1)], f"rag{n}")
        rows = cnew[n].reshape(ROWS, W)
        half = half + half_sq(rows)
        for i in range(YLO):
            b = i if n < NC - 1 else lax.rem(2 - 2 * c + i, YLO)
            start = b * NV if n < NC - 1 else pl.multiple_of(b * NV, NV)
            term = nt(rows, vall[pl.ds(start, NV), n * W : (n + 1) * W])
            if n > 0:
                term = lbuf[b] + term
            if n < NC - 1:
                lbuf[b] = term
            else:
                logits = SCALE * (term - half)
                peak = jnp.max(logits, axis=0, keepdims=True)
                expo = jnp.exp(logits - peak)
                lbuf[b] = expo
                core2[0, b, 0:1, :] = peak
                core2[0, b, 1:2, :] = jnp.sum(expo, axis=0, keepdims=True)
                if i == 1:
                    send(core2.at[0, theirs], core2.at[1, theirs], "core2", "core2", dc=1)

    wait(core2.at[1, pair], "rcore2")
    found = [
        merge([(core2[k, 2 * c + j, 0:1, :], core2[k, 2 * c + j, 1:2, :]) for k in range(2)]) for j in range(2)
    ]
    for s in range(2):
        turn = lax.rem(c + s, 2)
        at = y * (1 - turn) + z * turn
        for j in range(2):
            st2[s, at, j, 0:1, :], st2[s, at, j, 1:2, :] = found[j]
        for k in FARTHEST:
            send(st2.at[s, at], st2.at[s, at], f"st{s}", f"st{s}", dy=k * (1 - turn), dz=k * turn)
        wait(st2.at[s, pl.ds(0, NY - 1)], f"rst{s}")
        found = [merge([(st2[s, k, j, 0:1, :], st2[s, k, j, 1:2, :]) for k in range(NY)]) for j in range(2)]
    for j in range(2):
        fst2[2 * c + j, 0:1, :], fst2[2 * c + j, 1:2, :] = found[j]
    send(fst2.at[pair], fst2.at[pair], "core3", "core3", dc=1)

    others = [2 - 2 * c, 3 - 2 * c]
    for b in [2 * c, 2 * c + 1, *others]:
        if b is others[0]:
            acc[...] = weigh(2 * c, 0) + weigh(2 * c + 1, 0)
            wait(fst2.at[theirs], "rcore3")
        peak, total = fst2[b, 0:1, :], fst2[b, 1:2, :]
        share = jnp.exp(core2[0, b, 0:1, :] - peak) * (1.0 / total)
        resp[b] = (lbuf[b] * share).astype(BF16)

    def finish(n, fresh):
        out[:, n * W : (n + 1) * W] = fresh

    reduce(1, others, lambda n: cnew[n, x], finish)
    norm = fst2[q, 0:1, :] + jnp.log(fst2[q, 1:2, :])
    for k in range(NV // 128):
        logn[k : k + 1, :] = norm[:, k * 128 : (k + 1) * 128]

    landed(GATHER, "sgather")
    wait(core1.at[0], "score1")
    wait(zst1.at[pl.ds(0, NZ - 1)], "szst")
    wait(yst1.at[pl.ds(0, NY - 1)], "syst")
    for it in range(2):
        wait(rbuf.at[it, pl.ds(0, NX - 1)], f"srs{it}")
        wait(mbuf.at[it, pl.ds(0, NX - 1)], f"sm{it}")
        wait(st2.at[it, pl.ds(0, NY - 1)], f"sst{it}")
    wait(cnew.at[pl.ds(0, NX - 1)], "sag")
    wait(core2.at[0, pair], "score2")
    wait(fst2.at[pair], "score3")
    assert len(names) == SEMS, len(names)


def shards(vectors, centroids):
    result, log_norm = pl.pallas_call(
        kernel,
        out_shape=(
            jax.ShapeDtypeStruct((OWN, D), BF16),
            jax.ShapeDtypeStruct((NV // 128, 128), F32),
        ),
        in_specs=[pl.BlockSpec(memory_space=pl.ANY)] * 2,
        out_specs=(pl.BlockSpec(memory_space=pltpu.VMEM),) * 2,
        scratch_shapes=[
            pltpu.VMEM((YLO * NV, D), BF16),
            pltpu.VMEM((4 * ROWS, D), BF16),
            pltpu.VMEM((NC, NX, OWN, W), BF16),
            pltpu.VMEM((YLO, ROWS, NV), F32),
            pltpu.VMEM((YLO, ROWS, NV), BF16),
            pltpu.VMEM((ROWS, W), F32),
            pltpu.VMEM((2, NC, NX, OWN, W), BF16),
            pltpu.VMEM((2, NC, NX, OWN, W), BF16),
            pltpu.VMEM((2, NX, 1, ROWS), F32),
            pltpu.VMEM((ROWS, 128), F32),
            pltpu.VMEM((2, 2, NV), F32),
            pltpu.VMEM((NZ, 2, NV), F32),
            pltpu.VMEM((NY, 2, NV), F32),
            pltpu.VMEM((2, YLO, 2, NV), F32),
            pltpu.VMEM((2, NY, 2, 2, NV), F32),
            pltpu.VMEM((YLO, 2, NV), F32),
            pltpu.SemaphoreType.DMA((SEMS,)),
            pltpu.SemaphoreType.REGULAR((2,)),
        ],
        compiler_params=pltpu.CompilerParams(
            collective_id=0, has_side_effects=True, vmem_limit_bytes=54272 * 2**10
        ),
    )(vectors, centroids)
    return result, log_norm.reshape(NV)


def solution(mesh):
    in_specs = (P("item", None), P("cent", None))
    out_specs = (P(("cent", "item"), None), P("item"))
    return jax.shard_map(shards, mesh=mesh, in_specs=in_specs, out_specs=out_specs, check_vma=False)
```

```python
import functools
import math

import jax
import jax.numpy as jnp
from jax import lax
from jax.experimental import pallas as pl
from jax.experimental.pallas import tpu as pltpu
from jax.sharding import PartitionSpec as P

MESH = pl.DeviceIdType.MESH
F32, BF16 = jnp.float32, jnp.bfloat16
BETA = 3.0
NX, NY, NZ, YLO = 4, 8, 8, 4
NV, D = 768, 1024
ROWS = 256
OWN = 64
NC = 4
W = D // NC
HALF = NV // 2
STEPS = 48, 32
PART, REST = 80, 32
GATHER = 2 * (3 * PART + 3 * REST + 3 * PART) + 3 * HALF
SEMS = 49
FARTHEST = (4, 3, 5, 2, 6, 1, 7)
SCALE = BETA / math.sqrt(D)


def nt(a, b):
    return lax.dot_general(a, b, (((1,), (1,)), ((), ())), preferred_element_type=F32)


def merge(pairs):
    peak = functools.reduce(jnp.maximum, [p for p, _ in pairs])
    return peak, sum(t * jnp.exp(p - peak) for p, t in pairs)


def rows_at(b):
    start = b * NV
    return pl.ds(start if isinstance(b, int) else pl.multiple_of(start, NV), NV)


def local_stats(logits):
    peak = jnp.max(logits, axis=0, keepdims=True)
    return peak, jnp.sum(jnp.exp(logits - peak), axis=0, keepdims=True)


def half_sq(rows):
    wide = rows.astype(F32)
    return 0.5 * jnp.sum(wide * wide, axis=1, keepdims=True)


def kernel(
    vec, cen, out, logn,
    vall, cvm, cnew, lbuf, resp, acc, wbuf, rbuf, mbuf, mcol,
    core1, zst1, yst1, core2, st2, fst2, sem, ready,
):
    item, cent = lax.axis_index("item"), lax.axis_index("cent")
    x, q = lax.rem(item, NX), item // NX
    z, yhi, c = cent // 4, lax.rem(cent // 2, 2), lax.rem(cent, 2)
    y = yhi * YLO + q
    names = {}

    def sem_of(name):
        return sem.at[names.setdefault(name, len(names))]

    ids = {}

    def dev(**to):
        if not all(isinstance(step, int) for step in to.values()):
            return dev_of(**to)
        key = tuple(to.items())
        if key not in ids:
            ids[key] = dev_of(**to)
        return ids[key]

    def dev_of(dx=0, dy=0, dz=0, dc=0):
        x2, y2 = lax.rem(x + dx + NX, NX), lax.rem(y + dy + NY, NY)
        z2, c2 = lax.rem(z + dz + NZ, NZ), lax.rem(c + dc, 2)
        return {"item": lax.rem(y2, YLO) * NX + x2, "cent": z2 * 4 + (y2 // YLO) * 2 + c2}

    def send(src, dst, group, arrived, **to):
        pltpu.make_async_remote_copy(
            src_ref=src, dst_ref=dst, send_sem=sem_of("s" + group), recv_sem=sem_of("r" + arrived),
            device_id=dev(**to), device_id_type=MESH,
        ).start()

    def wait(like, name):
        pltpu.make_async_copy(like, like, sem_of(name)).wait()

    barrier = pltpu.get_barrier_semaphore()
    around = [dict(dy=1), dict(dy=-1), dict(dz=1), dict(dz=-1), dict(dx=1), dict(dx=-1)]
    beyond = [dict(dy=2), dict(dy=-2), dict(dz=2), dict(dz=-2)]

    def tell(semaphore, peers):
        for to in peers:
            pl.semaphore_signal(semaphore, inc=1, device_id=dev(**to), device_id_type=MESH)

    tell(barrier, [dict(dc=1)] + around)
    mine = pl.ds(pl.multiple_of(q * NV, NV), NV)
    load_v = pltpu.make_async_copy(vec, vall.at[mine], sem_of("load_v"))
    load_c = pltpu.make_async_copy(cen, cvm, sem_of("load_c"))
    load_v.start()
    load_c.start()
    pl.semaphore_wait(barrier, 1 + len(around))

    par = lax.rem(z, 2)

    def rows_of(kind, high):
        if isinstance(kind, tuple):
            start, _ = rows_of(kind[0], high)
            return start + kind[1] * STEPS[0], STEPS[kind[1]]
        if kind == "rest":
            return c * HALF + 4 * PART + high * REST, REST
        share = par if kind == "own" else 1 - par
        return c * HALF + (2 * share + high) * PART, PART

    def piece(block, kind, high):
        start, n = rows_of(kind, high)
        b = lax.rem(q + block + YLO, YLO)
        return vall.at[pl.ds(pl.multiple_of(b * NV + start, 16), n)]

    def first(kind, high, arrived, **to):
        start, n = rows_of(kind, high)
        send(vec.at[pl.ds(pl.multiple_of(start, 16), n)], piece(0, kind, high), "gather", arrived, **to)

    def along(block, kind, high, arrived, **to):
        part = piece(block, kind, high)
        send(part, part, "gather", arrived, **to)

    def cross(block, kind, high):
        along(block, kind, high, "far" if block == 2 else "near", dc=1)

    def landed(n, name):
        wait(vall.at[pl.ds(0, n)], name)

    first("own", 0, "A", dy=1)
    first("own", 1, "A", dy=-1)
    first("own", 1, "B", dy=1)
    first("own", 0, "B", dy=-1)
    first("rest", 0, "C", dy=1)
    first("rest", 1, "C", dy=-1)
    tell(ready.at[0], around)
    load_v.wait()
    load_c.wait()

    def score(k, carry):
        rows = cvm[pl.ds(pl.multiple_of(k * ROWS, ROWS), ROWS), :]
        logits = SCALE * (nt(rows, vall[mine, :]) - half_sq(rows))
        lbuf[k] = logits
        return merge([carry, local_stats(logits)])

    carry = jnp.full((1, NV), -3.0e38, F32), jnp.zeros((1, NV), F32)
    carry = lax.fori_loop(0, 2, score, carry)
    pl.semaphore_wait(ready.at[0], len(around))
    tell(ready.at[1], beyond)
    peak, total = lax.fori_loop(2, 4, score, carry)
    core1[0, 0:1, :] = peak
    core1[0, 1:2, :] = total
    send(core1.at[0], core1.at[1], "core1", "core1", dc=1)
    landed(2 * PART, "rA")
    for h in range(2):
        along(-1, ("own", h), 0, f"F{h}", dy=1)
        along(1, ("own", h), 1, f"F{h}", dy=-1)
    along(-1, "own", 0, "Z0", dz=1)
    along(1, "own", 1, "Z0", dz=-1)
    first("rest", 1, "D", dy=1)
    first("rest", 0, "D", dy=-1)
    cross(-1, "own", 0)
    cross(1, "own", 1)
    wait(core1.at[1], "rcore1")
    peak, total = merge([(core1[k, 0:1, :], core1[k, 1:2, :]) for k in range(2)])
    zst1[z, 0:1, :] = peak
    zst1[z, 1:2, :] = total
    pl.semaphore_wait(ready.at[1], len(beyond))
    for k in FARTHEST:
        send(zst1.at[z], zst1.at[z], "zst", "zst", dz=k)

    landed(2 * PART, "rB")
    along(1, "own", 0, "Z1", dz=1)
    along(-1, "own", 1, "Z1", dz=-1)
    cross(-1, "own", 1)
    cross(1, "own", 0)

    wait(zst1.at[pl.ds(0, NZ - 1)], "rzst")
    peak, total = merge([(zst1[k, 0:1, :], zst1[k, 1:2, :]) for k in range(NZ)])
    yst1[y, 0:1, :] = peak
    yst1[y, 1:2, :] = total
    for k in FARTHEST:
        send(yst1.at[y], yst1.at[y], "yst", "yst", dy=k)

    for h in range(2):
        landed(2 * STEPS[h], f"rF{h}")
        along(2, ("own", h), 0, f"Y{h}", dz=1)
        along(2, ("own", h), 1, f"Y{h}", dz=-1)
    cross(2, "own", 0)
    cross(2, "own", 1)
    landed(2 * PART, "rZ0")
    cross(-1, "other", 0)
    cross(1, "other", 1)
    landed(2 * REST, "rC")
    along(-1, "rest", 0, "G", dy=1)
    along(1, "rest", 1, "G", dy=-1)
    cross(-1, "rest", 0)
    cross(1, "rest", 1)
    landed(2 * PART, "rZ1")
    cross(1, "other", 0)
    cross(-1, "other", 1)
    landed(2 * REST, "rD")
    cross(-1, "rest", 1)
    cross(1, "rest", 0)

    crow = pl.ds(pl.multiple_of(q * ROWS, ROWS), ROWS)
    half = half_sq(cvm[crow, :])

    def respond(block):
        b = lax.rem(q + block, YLO)
        peak, total = merge([(yst1[b + k, 0:1, :], yst1[b + k, 1:2, :]) for k in (0, YLO)])
        if block == 0:
            logits = lbuf[q]
        else:
            part = vall[pl.ds(pl.multiple_of(b * NV, NV), NV), :]
            logits = SCALE * (nt(cvm[crow, :], part) - half)
        resp[b] = (jnp.exp(logits - peak) * (1.0 / total)).astype(BF16)

    wait(yst1.at[pl.ds(0, NY - 1)], "ryst")
    respond(0)
    landed(2 * STEPS[0], "rY0")
    cross(2, ("other", 0), 0)
    cross(2, ("other", 0), 1)
    landed(2 * HALF, "rnear")
    respond(3)
    landed(2 * STEPS[1], "rY1")
    cross(2, ("other", 1), 0)
    cross(2, ("other", 1), 1)
    landed(2 * REST, "rG")
    cross(2, "rest", 0)
    cross(2, "rest", 1)
    respond(1)

    def weigh(b, n):
        part = vall[rows_at(b), n * W : (n + 1) * W]
        return jnp.dot(resp[b], part, preferred_element_type=F32)

    acc[...] = sum(weigh(lax.rem(q + k, YLO), 0) for k in (0, 3, 1))
    landed(HALF, "rfar")
    respond(2)

    own = pl.ds(pl.multiple_of(q * ROWS + x * OWN, OWN), OWN)
    own64 = pl.ds(pl.multiple_of(x * OWN, OWN), OWN)

    def reduce(it, late, old, emit):
        for n in range(NC):
            if n == 0:
                part = acc[...] + sum(weigh(b, 0) for b in late)
            else:
                part = sum(weigh(b, n) for b in range(YLO))
            wbuf[it, n] = part.astype(BF16).reshape(NX, OWN, W)
            rbuf[it, n, 0] = wbuf[it, n, x]
            for k in (2, 1, 3):
                send(
                    wbuf.at[it, n, lax.rem(x + k, NX)], rbuf.at[it, n, k],
                    f"rs{it}", f"rs{it}{n}", dx=k,
                )
            if n == 0:
                mass = sum(jnp.sum(resp[b].astype(F32), axis=1, keepdims=True) for b in range(YLO))
                mbuf[it, x] = jnp.transpose(jnp.broadcast_to(mass, (ROWS, 128)))[0:1, :]
                for k in range(1, NX):
                    send(mbuf.at[it, x], mbuf.at[it, x], f"m{it}", f"m{it}", dx=k)
        wait(mbuf.at[it, pl.ds(0, NX - 1)], f"rm{it}")
        row = sum(mbuf[it, k] for k in range(NX))
        mcol[...] = jnp.transpose(jnp.broadcast_to(row, (128, ROWS)))
        div = mcol[own64, 0:1] + 1.0
        for n in range(NC):
            wait(rbuf.at[it, n, pl.ds(1, NX - 1)], f"rrs{it}{n}")
            sums = sum(rbuf[it, n, k].astype(F32) for k in range(NX))
            emit(n, ((sums + old(n).astype(F32)) / div).astype(BF16))

    def spread(n, fresh):
        cnew[n, x] = fresh
        for k in (2, 1, 3):
            send(cnew.at[n, x], cnew.at[n, x], "ag", f"ag{n}", dx=k)

    reduce(0, [lax.rem(q + 2, YLO)], lambda n: cvm[own, n * W : (n + 1) * W], spread)

    half = jnp.zeros((ROWS, 1), F32)
    theirs = pl.ds(2 - 2 * c, 2)
    pair = pl.ds(2 * c, 2)
    for n in range(NC):
        wait(cnew.at[n, pl.ds(0, NX - 1)], f"rag{n}")
        rows = cnew[n].reshape(ROWS, W)
        half = half + half_sq(rows)
        for i in range(YLO):
            b = i if n < NC - 1 else lax.rem(2 - 2 * c + i, YLO)
            start = b * NV if n < NC - 1 else pl.multiple_of(b * NV, NV)
            term = nt(rows, vall[pl.ds(start, NV), n * W : (n + 1) * W])
            if n > 0:
                term = lbuf[b] + term
            if n < NC - 1:
                lbuf[b] = term
            else:
                logits = SCALE * (term - half)
                peak = jnp.max(logits, axis=0, keepdims=True)
                expo = jnp.exp(logits - peak)
                lbuf[b] = expo
                core2[0, b, 0:1, :] = peak
                core2[0, b, 1:2, :] = jnp.sum(expo, axis=0, keepdims=True)
                if i == 1:
                    send(core2.at[0, theirs], core2.at[1, theirs], "core2", "core2", dc=1)

    wait(core2.at[1, pair], "rcore2")
    found = [
        merge([(core2[k, 2 * c + j, 0:1, :], core2[k, 2 * c + j, 1:2, :]) for k in range(2)]) for j in range(2)
    ]
    for s in range(2):
        turn = lax.rem(c + s, 2)
        at = y * (1 - turn) + z * turn
        for j in range(2):
            st2[s, at, j, 0:1, :], st2[s, at, j, 1:2, :] = found[j]
        for k in FARTHEST:
            send(st2.at[s, at], st2.at[s, at], f"st{s}", f"st{s}", dy=k * (1 - turn), dz=k * turn)
        wait(st2.at[s, pl.ds(0, NY - 1)], f"rst{s}")
        found = [merge([(st2[s, k, j, 0:1, :], st2[s, k, j, 1:2, :]) for k in range(NY)]) for j in range(2)]
    for j in range(2):
        fst2[2 * c + j, 0:1, :], fst2[2 * c + j, 1:2, :] = found[j]
    send(fst2.at[pair], fst2.at[pair], "core3", "core3", dc=1)

    others = [2 - 2 * c, 3 - 2 * c]
    for b in [2 * c, 2 * c + 1, *others]:
        if b is others[0]:
            acc[...] = weigh(2 * c, 0) + weigh(2 * c + 1, 0)
            wait(fst2.at[theirs], "rcore3")
        peak, total = fst2[b, 0:1, :], fst2[b, 1:2, :]
        share = jnp.exp(core2[0, b, 0:1, :] - peak) * (1.0 / total)
        resp[b] = (lbuf[b] * share).astype(BF16)

    def finish(n, fresh):
        out[:, n * W : (n + 1) * W] = fresh

    reduce(1, others, lambda n: cnew[n, x], finish)
    norm = fst2[q, 0:1, :] + jnp.log(fst2[q, 1:2, :])
    for k in range(NV // 128):
        logn[k : k + 1, :] = norm[:, k * 128 : (k + 1) * 128]

    landed(GATHER, "sgather")
    wait(core1.at[0], "score1")
    wait(zst1.at[pl.ds(0, NZ - 1)], "szst")
    wait(yst1.at[pl.ds(0, NY - 1)], "syst")
    for it in range(2):
        wait(rbuf.at[it, pl.ds(0, NX - 1)], f"srs{it}")
        wait(mbuf.at[it, pl.ds(0, NX - 1)], f"sm{it}")
        wait(st2.at[it, pl.ds(0, NY - 1)], f"sst{it}")
    wait(cnew.at[pl.ds(0, NX - 1)], "sag")
    wait(core2.at[0, pair], "score2")
    wait(fst2.at[pair], "score3")
    assert len(names) == SEMS, len(names)


def shards(vectors, centroids):
    result, log_norm = pl.pallas_call(
        kernel,
        out_shape=(
            jax.ShapeDtypeStruct((OWN, D), BF16),
            jax.ShapeDtypeStruct((NV // 128, 128), F32),
        ),
        in_specs=[pl.BlockSpec(memory_space=pl.ANY)] * 2,
        out_specs=(pl.BlockSpec(memory_space=pltpu.VMEM),) * 2,
        scratch_shapes=[
            pltpu.VMEM((YLO * NV, D), BF16),
            pltpu.VMEM((4 * ROWS, D), BF16),
            pltpu.VMEM((NC, NX, OWN, W), BF16),
            pltpu.VMEM((YLO, ROWS, NV), F32),
            pltpu.VMEM((YLO, ROWS, NV), BF16),
            pltpu.VMEM((ROWS, W), F32),
            pltpu.VMEM((2, NC, NX, OWN, W), BF16),
            pltpu.VMEM((2, NC, NX, OWN, W), BF16),
            pltpu.VMEM((2, NX, 1, ROWS), F32),
            pltpu.VMEM((ROWS, 128), F32),
            pltpu.VMEM((2, 2, NV), F32),
            pltpu.VMEM((NZ, 2, NV), F32),
            pltpu.VMEM((NY, 2, NV), F32),
            pltpu.VMEM((2, YLO, 2, NV), F32),
            pltpu.VMEM((2, NY, 2, 2, NV), F32),
            pltpu.VMEM((YLO, 2, NV), F32),
            pltpu.SemaphoreType.DMA((SEMS,)),
            pltpu.SemaphoreType.REGULAR((2,)),
        ],
        compiler_params=pltpu.CompilerParams(
            collective_id=0, has_side_effects=True, vmem_limit_bytes=54272 * 2**10
        ),
    )(vectors, centroids)
    return result, log_norm.reshape(NV)


def solution(mesh):
    in_specs = (P("item", None), P("cent", None))
    out_specs = (P(("cent", "item"), None), P("item"))
    return jax.shard_map(shards, mesh=mesh, in_specs=in_specs, out_specs=out_specs, check_vma=False)
```

```python
import functools
import math

import jax
import jax.numpy as jnp
from jax import lax
from jax.experimental import pallas as pl
from jax.experimental.pallas import tpu as pltpu
from jax.sharding import PartitionSpec as P

MESH = pl.DeviceIdType.MESH
F32, BF16 = jnp.float32, jnp.bfloat16
BETA = 3.0
NX, NY, NZ, YLO = 4, 8, 8, 4
NV, D = 768, 1024
ROWS = 256
OWN = 64
NC = 4
W = D // NC
HALF = NV // 2
STEPS = 48, 32
PART, REST = 80, 32
GATHER = 2 * (3 * PART + 3 * REST + 3 * PART) + 3 * HALF
SEMS = 49
FARTHEST = (4, 3, 5, 2, 6, 1, 7)
SCALE = BETA / math.sqrt(D)


def nt(a, b):
    return lax.dot_general(a, b, (((1,), (1,)), ((), ())), preferred_element_type=F32)


def merge(pairs):
    peak = functools.reduce(jnp.maximum, [p for p, _ in pairs])
    return peak, sum(t * jnp.exp(p - peak) for p, t in pairs)


def rows_at(b):
    start = b * NV
    return pl.ds(start if isinstance(b, int) else pl.multiple_of(start, NV), NV)


def local_stats(logits):
    peak = jnp.max(logits, axis=0, keepdims=True)
    return peak, jnp.sum(jnp.exp(logits - peak), axis=0, keepdims=True)


def half_sq(rows):
    wide = rows.astype(F32)
    return 0.5 * jnp.sum(wide * wide, axis=1, keepdims=True)


def kernel(
    vec, cen, out, logn,
    vall, cvm, cnew, lbuf, resp, acc, wbuf, rbuf, mbuf, mcol,
    core1, zst1, yst1, core2, st2, fst2, sem, ready,
):
    item, cent = lax.axis_index("item"), lax.axis_index("cent")
    x, q = lax.rem(item, NX), item // NX
    z, yhi, c = cent // 4, lax.rem(cent // 2, 2), lax.rem(cent, 2)
    y = yhi * YLO + q
    names = {}

    def sem_of(name):
        return sem.at[names.setdefault(name, len(names))]

    ids = {}

    def dev(**to):
        if not all(isinstance(step, int) for step in to.values()):
            return dev_of(**to)
        key = tuple(to.items())
        if key not in ids:
            ids[key] = dev_of(**to)
        return ids[key]

    def dev_of(dx=0, dy=0, dz=0, dc=0):
        x2, y2 = lax.rem(x + dx + NX, NX), lax.rem(y + dy + NY, NY)
        z2, c2 = lax.rem(z + dz + NZ, NZ), lax.rem(c + dc, 2)
        return {"item": lax.rem(y2, YLO) * NX + x2, "cent": z2 * 4 + (y2 // YLO) * 2 + c2}

    def send(src, dst, group, arrived, **to):
        pltpu.make_async_remote_copy(
            src_ref=src, dst_ref=dst, send_sem=sem_of("s" + group), recv_sem=sem_of("r" + arrived),
            device_id=dev(**to), device_id_type=MESH,
        ).start()

    def wait(like, name):
        pltpu.make_async_copy(like, like, sem_of(name)).wait()

    barrier = pltpu.get_barrier_semaphore()
    around = [dict(dy=1), dict(dy=-1), dict(dz=1), dict(dz=-1), dict(dx=1), dict(dx=-1)]
    beyond = [dict(dy=2), dict(dy=-2), dict(dz=2), dict(dz=-2)]

    def tell(semaphore, peers):
        for to in peers:
            pl.semaphore_signal(semaphore, inc=1, device_id=dev(**to), device_id_type=MESH)

    tell(barrier, [dict(dc=1)] + around)
    mine = pl.ds(pl.multiple_of(q * NV, NV), NV)
    load_v = pltpu.make_async_copy(vec, vall.at[mine], sem_of("load_v"))
    load_c = pltpu.make_async_copy(cen, cvm, sem_of("load_c"))
    load_v.start()
    load_c.start()
    pl.semaphore_wait(barrier, 1 + len(around))
    tell(ready.at[0], around)

    par = lax.rem(z, 2)

    def rows_of(kind, high):
        if isinstance(kind, tuple):
            start, _ = rows_of(kind[0], high)
            return start + kind[1] * STEPS[0], STEPS[kind[1]]
        if kind == "rest":
            return c * HALF + 4 * PART + high * REST, REST
        share = par if kind == "own" else 1 - par
        return c * HALF + (2 * share + high) * PART, PART

    def piece(block, kind, high):
        start, n = rows_of(kind, high)
        b = lax.rem(q + block + YLO, YLO)
        return vall.at[pl.ds(pl.multiple_of(b * NV + start, 16), n)]

    def first(kind, high, arrived, **to):
        start, n = rows_of(kind, high)
        send(vec.at[pl.ds(pl.multiple_of(start, 16), n)], piece(0, kind, high), "gather", arrived, **to)

    def along(block, kind, high, arrived, **to):
        part = piece(block, kind, high)
        send(part, part, "gather", arrived, **to)

    def cross(block, kind, high):
        along(block, kind, high, "far" if block == 2 else "near", dc=1)

    def landed(n, name):
        wait(vall.at[pl.ds(0, n)], name)

    first("own", 0, "A", dy=1)
    first("own", 1, "A", dy=-1)
    first("own", 1, "B", dy=1)
    first("own", 0, "B", dy=-1)
    first("rest", 0, "C", dy=1)
    first("rest", 1, "C", dy=-1)
    load_v.wait()
    load_c.wait()

    def score(k, carry):
        rows = cvm[pl.ds(pl.multiple_of(k * ROWS, ROWS), ROWS), :]
        logits = SCALE * (nt(rows, vall[mine, :]) - half_sq(rows))
        lbuf[k] = logits
        return merge([carry, local_stats(logits)])

    carry = jnp.full((1, NV), -3.0e38, F32), jnp.zeros((1, NV), F32)
    carry = lax.fori_loop(0, 2, score, carry)
    pl.semaphore_wait(ready.at[0], len(around))
    tell(ready.at[1], beyond)
    peak, total = lax.fori_loop(2, 4, score, carry)
    core1[0, 0:1, :] = peak
    core1[0, 1:2, :] = total
    send(core1.at[0], core1.at[1], "core1", "core1", dc=1)
    wait(core1.at[1], "rcore1")
    peak, total = merge([(core1[k, 0:1, :], core1[k, 1:2, :]) for k in range(2)])
    zst1[z, 0:1, :] = peak
    zst1[z, 1:2, :] = total
    pl.semaphore_wait(ready.at[1], len(beyond))
    for k in FARTHEST:
        send(zst1.at[z], zst1.at[z], "zst", "zst", dz=k)

    landed(2 * PART, "rA")
    for h in range(2):
        along(-1, ("own", h), 0, f"F{h}", dy=1)
        along(1, ("own", h), 1, f"F{h}", dy=-1)
    along(-1, "own", 0, "Z0", dz=1)
    along(1, "own", 1, "Z0", dz=-1)
    first("rest", 1, "D", dy=1)
    first("rest", 0, "D", dy=-1)
    cross(-1, "own", 0)
    cross(1, "own", 1)
    landed(2 * PART, "rB")
    along(1, "own", 0, "Z1", dz=1)
    along(-1, "own", 1, "Z1", dz=-1)
    cross(-1, "own", 1)
    cross(1, "own", 0)

    wait(zst1.at[pl.ds(0, NZ - 1)], "rzst")
    peak, total = merge([(zst1[k, 0:1, :], zst1[k, 1:2, :]) for k in range(NZ)])
    yst1[y, 0:1, :] = peak
    yst1[y, 1:2, :] = total
    for k in FARTHEST:
        send(yst1.at[y], yst1.at[y], "yst", "yst", dy=k)

    for h in range(2):
        landed(2 * STEPS[h], f"rF{h}")
        along(2, ("own", h), 0, f"Y{h}", dz=1)
        along(2, ("own", h), 1, f"Y{h}", dz=-1)
    cross(2, "own", 0)
    cross(2, "own", 1)
    landed(2 * PART, "rZ0")
    cross(-1, "other", 0)
    cross(1, "other", 1)
    landed(2 * REST, "rC")
    along(-1, "rest", 0, "G", dy=1)
    along(1, "rest", 1, "G", dy=-1)
    cross(-1, "rest", 0)
    cross(1, "rest", 1)
    landed(2 * PART, "rZ1")
    cross(1, "other", 0)
    cross(-1, "other", 1)
    landed(2 * REST, "rD")
    cross(-1, "rest", 1)
    cross(1, "rest", 0)

    crow = pl.ds(pl.multiple_of(q * ROWS, ROWS), ROWS)
    half = half_sq(cvm[crow, :])

    def respond(block):
        b = lax.rem(q + block, YLO)
        peak, total = merge([(yst1[b + k, 0:1, :], yst1[b + k, 1:2, :]) for k in (0, YLO)])
        if block == 0:
            logits = lbuf[q]
        else:
            part = vall[pl.ds(pl.multiple_of(b * NV, NV), NV), :]
            logits = SCALE * (nt(cvm[crow, :], part) - half)
        resp[b] = (jnp.exp(logits - peak) * (1.0 / total)).astype(BF16)

    wait(yst1.at[pl.ds(0, NY - 1)], "ryst")
    respond(0)
    landed(2 * STEPS[0], "rY0")
    cross(2, ("other", 0), 0)
    cross(2, ("other", 0), 1)
    landed(2 * HALF, "rnear")
    respond(3)
    landed(2 * STEPS[1], "rY1")
    cross(2, ("other", 1), 0)
    cross(2, ("other", 1), 1)
    landed(2 * REST, "rG")
    cross(2, "rest", 0)
    cross(2, "rest", 1)
    respond(1)

    def weigh(b, n):
        part = vall[rows_at(b), n * W : (n + 1) * W]
        return jnp.dot(resp[b], part, preferred_element_type=F32)

    acc[...] = sum(weigh(lax.rem(q + k, YLO), 0) for k in (0, 3, 1))
    landed(HALF, "rfar")
    respond(2)

    own = pl.ds(pl.multiple_of(q * ROWS + x * OWN, OWN), OWN)
    own64 = pl.ds(pl.multiple_of(x * OWN, OWN), OWN)

    def reduce(it, late, old, emit, meanwhile=None):
        for n in range(NC):
            if n == 0:
                part = acc[...] + sum(weigh(b, 0) for b in late)
            else:
                part = sum(weigh(b, n) for b in range(YLO))
            wbuf[it, n] = part.astype(BF16).reshape(NX, OWN, W)
            rbuf[it, n, 0] = wbuf[it, n, x]
            for k in (2, 1, 3):
                send(
                    wbuf.at[it, n, lax.rem(x + k, NX)], rbuf.at[it, n, k],
                    f"rs{it}", f"rs{it}{n}", dx=k,
                )
            if n == 0:
                mass = sum(jnp.sum(resp[b].astype(F32), axis=1, keepdims=True) for b in range(YLO))
                mbuf[it, x] = jnp.transpose(jnp.broadcast_to(mass, (ROWS, 128)))[0:1, :]
                for k in range(1, NX):
                    send(mbuf.at[it, x], mbuf.at[it, x], f"m{it}", f"m{it}", dx=k)
        if meanwhile is not None:
            meanwhile()
        wait(mbuf.at[it, pl.ds(0, NX - 1)], f"rm{it}")
        row = sum(mbuf[it, k] for k in range(NX))
        mcol[...] = jnp.transpose(jnp.broadcast_to(row, (128, ROWS)))
        div = mcol[own64, 0:1] + 1.0
        for n in range(NC):
            wait(rbuf.at[it, n, pl.ds(1, NX - 1)], f"rrs{it}{n}")
            sums = sum(rbuf[it, n, k].astype(F32) for k in range(NX))
            emit(n, ((sums + old(n).astype(F32)) / div).astype(BF16))

    def spread(n, fresh):
        cnew[n, x] = fresh
        for k in (2, 1, 3):
            send(cnew.at[n, x], cnew.at[n, x], "ag", f"ag{n}", dx=k)

    reduce(0, [lax.rem(q + 2, YLO)], lambda n: cvm[own, n * W : (n + 1) * W], spread)

    half = jnp.zeros((ROWS, 1), F32)
    theirs = pl.ds(2 - 2 * c, 2)
    pair = pl.ds(2 * c, 2)
    for n in range(NC):
        wait(cnew.at[n, pl.ds(0, NX - 1)], f"rag{n}")
        rows = cnew[n].reshape(ROWS, W)
        half = half + half_sq(rows)
        for i in range(YLO):
            b = i if n < NC - 1 else lax.rem(2 - 2 * c + i, YLO)
            start = b * NV if n < NC - 1 else pl.multiple_of(b * NV, NV)
            term = nt(rows, vall[pl.ds(start, NV), n * W : (n + 1) * W])
            if n > 0:
                term = lbuf[b] + term
            if n < NC - 1:
                lbuf[b] = term
            else:
                logits = SCALE * (term - half)
                peak = jnp.max(logits, axis=0, keepdims=True)
                expo = jnp.exp(logits - peak)
                lbuf[b] = expo
                core2[0, b, 0:1, :] = peak
                core2[0, b, 1:2, :] = jnp.sum(expo, axis=0, keepdims=True)
                if i == 1:
                    send(core2.at[0, theirs], core2.at[1, theirs], "core2", "core2", dc=1)

    wait(core2.at[1, pair], "rcore2")
    found = [
        merge([(core2[k, 2 * c + j, 0:1, :], core2[k, 2 * c + j, 1:2, :]) for k in range(2)]) for j in range(2)
    ]
    for s in range(2):
        turn = lax.rem(c + s, 2)
        at = y * (1 - turn) + z * turn
        for j in range(2):
            st2[s, at, j, 0:1, :], st2[s, at, j, 1:2, :] = found[j]
        for k in FARTHEST:
            send(st2.at[s, at], st2.at[s, at], f"st{s}", f"st{s}", dy=k * (1 - turn), dz=k * turn)
        wait(st2.at[s, pl.ds(0, NY - 1)], f"rst{s}")
        found = [merge([(st2[s, k, j, 0:1, :], st2[s, k, j, 1:2, :]) for k in range(NY)]) for j in range(2)]
    for j in range(2):
        fst2[2 * c + j, 0:1, :], fst2[2 * c + j, 1:2, :] = found[j]
    send(fst2.at[pair], fst2.at[pair], "core3", "core3", dc=1)

    others = [2 - 2 * c, 3 - 2 * c]
    for b in [2 * c, 2 * c + 1, *others]:
        if b is others[0]:
            acc[...] = weigh(2 * c, 0) + weigh(2 * c + 1, 0)
            wait(fst2.at[theirs], "rcore3")
        peak, total = fst2[b, 0:1, :], fst2[b, 1:2, :]
        share = jnp.exp(core2[0, b, 0:1, :] - peak) * (1.0 / total)
        resp[b] = (lbuf[b] * share).astype(BF16)

    def finish(n, fresh):
        out[:, n * W : (n + 1) * W] = fresh

    def left(it):
        wait(rbuf.at[it, pl.ds(0, NX - 1)], f"srs{it}")
        wait(mbuf.at[it, pl.ds(0, NX - 1)], f"sm{it}")

    def close():
        norm = fst2[q, 0:1, :] + jnp.log(fst2[q, 1:2, :])
        for k in range(NV // 128):
            logn[k : k + 1, :] = norm[:, k * 128 : (k + 1) * 128]
        landed(GATHER, "sgather")
        wait(core1.at[0], "score1")
        wait(zst1.at[pl.ds(0, NZ - 1)], "szst")
        wait(yst1.at[pl.ds(0, NY - 1)], "syst")
        for k in range(2):
            wait(st2.at[k, pl.ds(0, NY - 1)], f"sst{k}")
        wait(cnew.at[pl.ds(0, NX - 1)], "sag")
        wait(core2.at[0, pair], "score2")
        wait(fst2.at[pair], "score3")
        left(0)

    reduce(1, others, lambda n: cnew[n, x], finish, close)
    left(1)
    assert len(names) == SEMS, len(names)


def shards(vectors, centroids):
    result, log_norm = pl.pallas_call(
        kernel,
        out_shape=(
            jax.ShapeDtypeStruct((OWN, D), BF16),
            jax.ShapeDtypeStruct((NV // 128, 128), F32),
        ),
        in_specs=[pl.BlockSpec(memory_space=pl.ANY)] * 2,
        out_specs=(pl.BlockSpec(memory_space=pltpu.VMEM),) * 2,
        scratch_shapes=[
            pltpu.VMEM((YLO * NV, D), BF16),
            pltpu.VMEM((4 * ROWS, D), BF16),
            pltpu.VMEM((NC, NX, OWN, W), BF16),
            pltpu.VMEM((YLO, ROWS, NV), F32),
            pltpu.VMEM((YLO, ROWS, NV), BF16),
            pltpu.VMEM((ROWS, W), F32),
            pltpu.VMEM((2, NC, NX, OWN, W), BF16),
            pltpu.VMEM((2, NC, NX, OWN, W), BF16),
            pltpu.VMEM((2, NX, 1, ROWS), F32),
            pltpu.VMEM((ROWS, 128), F32),
            pltpu.VMEM((2, 2, NV), F32),
            pltpu.VMEM((NZ, 2, NV), F32),
            pltpu.VMEM((NY, 2, NV), F32),
            pltpu.VMEM((2, YLO, 2, NV), F32),
            pltpu.VMEM((2, NY, 2, 2, NV), F32),
            pltpu.VMEM((YLO, 2, NV), F32),
            pltpu.SemaphoreType.DMA((SEMS,)),
            pltpu.SemaphoreType.REGULAR((2,)),
        ],
        compiler_params=pltpu.CompilerParams(
            collective_id=0, has_side_effects=True, vmem_limit_bytes=54272 * 2**10
        ),
    )(vectors, centroids)
    return result, log_norm.reshape(NV)


def solution(mesh):
    in_specs = (P("item", None), P("cent", None))
    out_specs = (P(("cent", "item"), None), P("item"))
    return jax.shard_map(shards, mesh=mesh, in_specs=in_specs, out_specs=out_specs, check_vma=False)
```
